256 devices in a mesh: seq: 64 (over z_lo, y, x), chan: 4 (over z_hi, core).
Axes of the slice: x: 4, y: 4, z: 8 (z_hi: 2, z_lo: 4; z = z_hi * 4 + z_lo), core: 2. Of those that a mesh axis runs over, the one named last changes fastest.
Arguments:
- residual: bfloat16 [8192, 4096], P('seq', 'chan'), may hold values from -40 to 40
- query_feats: bfloat16 [8192, 4096], P('seq', 'chan'), may hold values from -6 to 6
- key_feats: bfloat16 [8192, 4096], P('seq', 'chan'), may hold values from -6 to 6
- value_feats: bfloat16 [8192, 4096], P('seq', 'chan'), may hold values from -6 to 6
- filters: bfloat16 [8192, 4096], P('seq', 'chan'), may hold values from -1 to 1
- cotangent: bfloat16 [8192, 4096], P('seq', 'chan'), may hold values from -12 to 12
- skip_bias: float32 [4096], P('chan'), may hold values from -1 to 1
- norm_gain: float32 [4096], P('chan'), may hold values from 0.5 to 1.5
Outputs:
- normed: bfloat16 [8192, 4096], P('seq', 'chan')
- grad_residual: bfloat16 [8192, 4096], P('seq', 'chan')
- grad_query: bfloat16 [8192, 4096], P('seq', 'chan')
- grad_key: bfloat16 [8192, 4096], P('seq', 'chan')
- grad_value: bfloat16 [8192, 4096], P('seq', 'chan')
- grad_filter: float32 [8192, 4096], P('seq', 'chan')
- grad_bias: float32 [4096], P('chan')
- grad_gain: float32 [4096], P('chan')
The draws below stay inside these ranges and needn't reach their ends.
All inputs are finite; a program needn't handle non-finite values.
Results may differ from the reference program's by a relative error of at most 0.007.
Values may be sent and summed in bfloat16 or wider, within the bound.
No kernel may reach another device: no remote copies, remote signals or barrier semaphores. Data moves between devices by JAX's collectives and lax.ppermute only.
A program may use at most 64 MiB of HBM per device.

```python
import math
import jax
import jax.numpy as jnp
from jax import lax

D = 4096
SEQUENCE_LENGTH = 8192


def draw_residual(key, part):
    key = jax.random.fold_in(key, 11)
    jitter_random_key, row_key, col_key = jax.random.split(key, 3)
    row_scale = 0.3 * jnp.exp(math.log(10.0) * jax.random.uniform(row_key, (SEQUENCE_LENGTH, 1)))
    channel_ramp = jnp.arange(D, dtype=jnp.float32)[None, :] / (D - 1)
    col_scale = 0.3 * jnp.exp(math.log(10.0) * (0.5 * channel_ramp + 0.5 * jax.random.uniform(col_key, (1, D))))
    noise_part = jax.random.truncated_normal(jitter_random_key, -4.0, 4.0, (SEQUENCE_LENGTH, D))
    return (noise_part * row_scale * col_scale).astype(jnp.bfloat16)


def draw_filters(key, part):
    key = jax.random.fold_in(key, 23)
    interval_random_key, spike_random_key, jitter_random_key = jax.random.split(key, 3)
    lowest = math.log(32.0)
    spans = jnp.exp(jax.random.uniform(interval_random_key, (1, D), minval=lowest, maxval=math.log(4.0 * SEQUENCE_LENGTH)))
    device_slots = jax.random.randint(spike_random_key, (1, 1, 3), 1, SEQUENCE_LENGTH)
    lag_index = jnp.arange(SEQUENCE_LENGTH, dtype=jnp.int32)[:, None, None]
    drops = jnp.sum((lag_index >= device_slots).astype(jnp.float32), axis=2)
    lags = jnp.arange(SEQUENCE_LENGTH, dtype=jnp.float32)[:, None]
    envelope = jnp.exp(-lags / spans) * jnp.power(0.6, drops) * jnp.sqrt(2.0 / spans)
    noise_part = jax.random.truncated_normal(jitter_random_key, -4.0, 4.0, (SEQUENCE_LENGTH, D))
    return (noise_part * envelope).astype(jnp.bfloat16)


def draw_cotangent(key, part):
    key = jax.random.fold_in(key, 37)
    place = jnp.arange(SEQUENCE_LENGTH, dtype=jnp.float32)[:, None] / (SEQUENCE_LENGTH - 1)
    noise_part = jax.random.truncated_normal(key, -4.0, 4.0, (SEQUENCE_LENGTH, D))
    token_ramp = 1.0 + 2.0 * place
    return (noise_part * token_ramp).astype(jnp.bfloat16)


def block_levels(stream_key, extent, cuts, least, high):
    loudness, own = 1.0, jax.random.fold_in(stream_key, 6)
    for dim, parts in cuts:
        draws = jnp.exp(jax.random.uniform(jax.random.fold_in(own, dim), (parts,), jnp.float32, least / len(cuts), high / len(cuts)))
        loudness = loudness * jnp.repeat(draws, extent[dim] // parts).reshape([-1 if axis == dim else 1 for axis in range(len(extent))])
    return loudness


def scatter_about(key, dims, scale, limit, pieces=(), held_as=jnp.bfloat16):
    level = block_levels(key, dims, pieces, -0.22, 0.18) if pieces else 1.0
    values = jax.random.normal(key, dims, jnp.float32) * scale * level
    return jnp.minimum(jnp.maximum(values, -limit), limit).astype(held_as)


def setup_inputs(seed: int = 0) -> dict:
    splits = jax.random.split(jax.random.key(seed), 9)
    residual = draw_residual(jax.random.fold_in(splits[8], 71), 0)
    query_feats = scatter_about(splits[1], (SEQUENCE_LENGTH, D), 1.0, 6.0, ((0, 64), (1, 4)))
    key_feats = scatter_about(splits[2], (SEQUENCE_LENGTH, D), 1.0, 6.0, ((0, 64), (1, 4)))
    value_feats = scatter_about(splits[3], (SEQUENCE_LENGTH, D), 1.0, 6.0, ((0, 64), (1, 4)))
    filters = draw_filters(jax.random.fold_in(splits[8], 71), 0)
    cotangent = draw_cotangent(jax.random.fold_in(splits[8], 71), 0)
    skip_bias = jnp.clip(jax.random.uniform(splits[6], (D,), jnp.float32, -1.0, 1.0) * block_levels(splits[6], (D,), ((0, 4),), -0.4, 0.0), -1.0, 1.0)
    norm_gain = jnp.clip(1.0 + 0.1 * jax.random.normal(splits[7], (D,), jnp.float32), 0.5, 1.5)
    return dict(residual=residual, query_feats=query_feats, key_feats=key_feats, value_feats=value_feats, filters=filters, cotangent=cotangent, skip_bias=skip_bias, norm_gain=norm_gain)


epsilon = 1e-06

def causal_block(first, second):
    length = first.shape[0]
    spectrum = jnp.fft.rfft(first, n=2 * length, axis=0) * jnp.fft.rfft(second, n=2 * length, axis=0)
    return jnp.fft.irfft(spectrum, n=2 * length, axis=0)[:length].astype(jnp.float32)

def lagged_block(first, second):
    length = first.shape[0]
    spectrum = jnp.conj(jnp.fft.rfft(first, n=2 * length, axis=0)) * jnp.fft.rfft(second, n=2 * length, axis=0)
    return jnp.fft.irfft(spectrum, n=2 * length, axis=0)[:length].astype(jnp.float32)

def by_channels(kernel, first, second):
    length, width = first.shape
    stride = math.gcd(width, 256)
    left_side = first.reshape(length, width // stride, stride).transpose(1, 0, 2)
    right_side = second.reshape(length, width // stride, stride).transpose(1, 0, 2)

    def apply_pair(operands):
        return kernel(operands[0], operands[1])
    result = lax.map(apply_pair, (left_side, right_side))
    return result.transpose(1, 0, 2).reshape(length, width)

def reference(residual, query_feats, key_feats, value_feats, filters, cotangent, skip_bias, norm_gain):
    query_wide = query_feats.astype(jnp.float32)
    key_wide = key_feats.astype(jnp.float32)
    value_wide = value_feats.astype(jnp.float32)
    filter_broadcast = filters.astype(jnp.float32)
    product = (key_wide * value_wide).astype(jnp.bfloat16)
    product_wide = product.astype(jnp.float32)
    conv = by_channels(causal_block, filter_broadcast, product_wide)
    mixed = conv + skip_bias[None, :] * product_wide
    summed = residual.astype(jnp.float32) + query_wide * mixed
    inv_rms = lax.rsqrt(lax.optimization_barrier(jnp.mean(summed * summed, axis=1)) + epsilon)
    normed = (summed * inv_rms[:, None] * norm_gain[None, :]).astype(jnp.bfloat16)
    grad_wide = cotangent.astype(jnp.float32)
    scaled_grad = grad_wide * norm_gain[None, :]
    inner_sum = lax.optimization_barrier(jnp.sum(scaled_grad * summed, axis=1))
    grad_summed = inv_rms[:, None] * scaled_grad - summed * (inv_rms ** 3 * inner_sum / D)[:, None]
    grad_residual = grad_summed.astype(jnp.bfloat16)
    grad_query = (grad_summed * mixed).astype(jnp.bfloat16)
    grad_mixed = (grad_summed * query_wide).astype(jnp.bfloat16)
    mixed_back = grad_mixed.astype(jnp.float32)
    back_conv = by_channels(lagged_block, filter_broadcast, mixed_back)
    grad_product = back_conv + skip_bias[None, :] * mixed_back
    grad_key = (grad_product * value_wide).astype(jnp.bfloat16)
    grad_value = (grad_product * key_wide).astype(jnp.bfloat16)
    grad_filter = by_channels(lagged_block, product_wide, mixed_back)
    grad_bias = lax.optimization_barrier(jnp.sum(mixed_back * product_wide, axis=0))
    grad_gain = lax.optimization_barrier(jnp.sum(grad_wide * summed * inv_rms[:, None], axis=0))
    return (normed, grad_residual, grad_query, grad_key, grad_value, grad_filter, grad_bias, grad_gain)
```

```python
import functools
import math

import jax
import jax.numpy as jnp
import ml_dtypes
import numpy as np
from jax import lax
from jax.experimental import pallas as pl
from jax.experimental.pallas import tpu as pltpu
from jax.sharding import PartitionSpec as P

epsilon = 1e-06
f32 = jnp.float32
bf16 = jnp.bfloat16


def split_host(table):
    high = table.astype(ml_dtypes.bfloat16)
    low = (table - high.astype(np.float64)).astype(ml_dtypes.bfloat16)
    return high, low


@functools.cache
def tables(blocks, lanes):
    length = 2 * blocks * lanes
    k1 = np.arange(blocks)[:, None] + 0.5
    a = np.arange(blocks)[None, :]
    angle = 2.0 * np.pi * k1 * a / (2 * blocks)
    outer = np.concatenate((np.cos(angle), -np.sin(angle)), 0)
    outer_high, outer_low = split_host(outer)
    first = np.concatenate((outer_high, outer_low), 1)
    back = outer.T * (2.0 / length)
    back_high, back_low = split_host(back)
    last = np.concatenate((back_high, back_low, back_high), 1)
    b = np.arange(lanes)[None, :]
    angle = 2.0 * np.pi * k1 * b / length
    twiddle = np.concatenate((np.cos(angle), np.sin(angle)), 0).astype(np.float32)
    angle = 2.0 * np.pi * (np.arange(lanes)[:, None] * b % lanes) / lanes
    cosine, sine = np.cos(angle), np.sin(angle)
    inner = np.block([[cosine, -sine], [sine, cosine]])
    inner_high, inner_low = split_host(inner)
    inverse_high, inverse_low = split_host(inner.T)
    return (first, last, twiddle, inner_high, inner_low, inverse_high, inverse_low)


def split(values):
    high = values.astype(bf16)
    low = (values - high.astype(f32)).astype(bf16)
    return high, low


def matmul(left, right):
    return jnp.dot(left, right, preferred_element_type=f32)


def forward(series_ref, stride, rows, first_ref, twiddle_ref, high_ref, low_ref, uh_ref, ul_ref):
    blocks = first_ref.shape[0] // 2
    lanes = twiddle_ref.shape[1]
    cosine = twiddle_ref[:blocks]
    sine = twiddle_ref[blocks:]
    for pair in range(rows // 2):
        columns = []
        for row in (2 * pair, 2 * pair + 1):
            x = series_ref[pl.ds(row, blocks, stride=stride), :].astype(bf16)
            columns.append(jnp.concatenate((x, x), 0))
        out = matmul(first_ref[...], jnp.concatenate(columns, 1))
        for i in range(2):
            re = out[:blocks, i * lanes : (i + 1) * lanes]
            im = out[blocks:, i * lanes : (i + 1) * lanes]
            here = pl.ds((2 * pair + i) * blocks, blocks)
            uh, ul = split(re * cosine + im * sine)
            uh_ref[here, :lanes] = uh
            ul_ref[here, :lanes] = ul
            uh, ul = split(im * cosine - re * sine)
            uh_ref[here, lanes:] = uh
            ul_ref[here, lanes:] = ul
    count = rows * blocks
    uh, ul = uh_ref[:count], ul_ref[:count]
    return matmul(uh, high_ref[...]) + matmul(ul, high_ref[...]) + matmul(uh, low_ref[...])


def inverse(rows, last_ref, twiddle_ref, high_ref, low_ref, uh_ref, ul_ref, z_ref, out_ref, stride):
    blocks = last_ref.shape[0]
    lanes = twiddle_ref.shape[1]
    cosine = twiddle_ref[:blocks]
    sine = twiddle_ref[blocks:]
    count = rows * blocks
    uh, ul = uh_ref[:count], ul_ref[:count]
    z_ref[:count] = matmul(uh, high_ref[...]) + matmul(ul, high_ref[...]) + matmul(uh, low_ref[...])
    for pair in range(rows // 2):
        columns = []
        for row in (2 * pair, 2 * pair + 1):
            re = z_ref[pl.ds(row * blocks, blocks), :lanes]
            im = z_ref[pl.ds(row * blocks, blocks), lanes:]
            zh, zl = split(
                jnp.concatenate((re * cosine - im * sine, im * cosine + re * sine), 0)
            )
            columns.append(jnp.concatenate((zh, zh, zl), 0))
        out = matmul(last_ref[...], jnp.concatenate(columns, 1))
        for i in range(2):
            out_ref[pl.ds(2 * pair + i, blocks, stride=stride), :] = out[
                :, i * lanes : (i + 1) * lanes
            ]


def conv_kernel(
    recv_ref, skip_ref, first_ref, last_ref, twiddle_ref, high_ref, low_ref, ihigh_ref, ilow_ref,
    mixed_ref, spec_ref, x_ref, uh_ref, ul_ref, z_ref, y_ref,
):
    blocks, rows, lanes = recv_ref.shape
    channels = rows // 2
    half = channels * blocks
    x_ref[...] = recv_ref[...].astype(f32).reshape(blocks * rows, lanes)
    spec_ref[...] = forward(
        x_ref, rows, rows, first_ref, twiddle_ref, high_ref, low_ref, uh_ref, ul_ref
    )
    for c in range(channels):
        prod = pl.ds(c * blocks, blocks)
        filt = pl.ds(half + c * blocks, blocks)
        fre = spec_ref[filt, :lanes] + skip_ref[c]
        spec_ref[filt, :lanes] = fre
        fim = spec_ref[filt, lanes:]
        pre, pim = spec_ref[prod, :lanes], spec_ref[prod, lanes:]
        uh_ref[prod, :lanes], ul_ref[prod, :lanes] = split(pre * fre - pim * fim)
        uh_ref[prod, lanes:], ul_ref[prod, lanes:] = split(pre * fim + pim * fre)
    inverse(
        channels, last_ref, twiddle_ref, ihigh_ref, ilow_ref, uh_ref, ul_ref, z_ref, y_ref, channels
    )
    mixed_ref[...] = y_ref[...].reshape(blocks, channels, lanes).astype(bf16)


def lag_kernel(
    recv_ref, spec_ref, first_ref, last_ref, twiddle_ref, high_ref, low_ref, ihigh_ref, ilow_ref,
    out_ref, x_ref, g_ref, uh_ref, ul_ref, z_ref, y_ref,
):
    blocks, rows, lanes = recv_ref.shape
    channels = rows // 2
    half = channels * blocks
    x_ref[...] = recv_ref[:, :channels, :].astype(f32).reshape(half, lanes)
    gain = jnp.sum(recv_ref[:, channels:, :].astype(f32), axis=0)
    gain = jnp.sum(gain, axis=1, keepdims=True) * (2.0 / lanes)
    g_ref[...] = forward(
        x_ref, channels, channels, first_ref, twiddle_ref, high_ref, low_ref, uh_ref, ul_ref
    )
    for c in range(channels):
        prod = pl.ds(c * blocks, blocks)
        filt = pl.ds(half + c * blocks, blocks)
        gre, gim = g_ref[prod, :lanes], g_ref[prod, lanes:]
        for source, target in ((filt, prod), (prod, filt)):
            sre, sim = spec_ref[source, :lanes], spec_ref[source, lanes:]
            uh_ref[target, :lanes], ul_ref[target, :lanes] = split(sre * gre + sim * gim)
            uh_ref[target, lanes:], ul_ref[target, lanes:] = split(sre * gim - sim * gre)
    inverse(
        rows, last_ref, twiddle_ref, ihigh_ref, ilow_ref, uh_ref, ul_ref, z_ref, y_ref, rows
    )
    out_ref[:, :rows, :] = y_ref[...].reshape(blocks, rows, lanes).astype(bf16)
    bias = y_ref[channels:rows, 0:1]
    lane = lax.broadcasted_iota(jnp.int32, (channels, lanes), 1)
    quarter = lanes // 4
    value = jnp.where(lane < 2 * quarter, bias, gain)
    vh = value.astype(bf16).astype(f32)
    value = jnp.where((lane // quarter) % 2 == 0, vh, value - vh).astype(bf16)
    out_ref[:, rows:, :] = jnp.broadcast_to(value[None], (blocks, channels, lanes))


def send_kernel(key_ref, value_ref, filters_ref, out_ref):
    tokens, width = key_ref.shape
    peers, rows, _ = out_ref.shape
    channels = rows // 2
    group = tokens // channels
    for j in range(width // tokens):
        cols = pl.ds(j * tokens, tokens)
        dest = pl.ds(j * group, group)
        product = key_ref[:, cols].astype(f32) * value_ref[:, cols].astype(f32)
        out_ref[dest, :channels, :] = product.astype(bf16).T.reshape(group, channels, tokens)
        out_ref[dest, channels:, :] = filters_ref[:, cols].T.reshape(group, channels, tokens)


def turn_kernel(residual_ref, query_ref, cotangent_ref, gain_ref, res_ref, q_ref, g_ref, sg_ref):
    tokens, width = residual_ref.shape
    for j in range(width // tokens):
        cols = pl.ds(j * tokens, tokens)
        res_ref[cols, :] = residual_ref[:, cols].T
        q_ref[cols, :] = query_ref[:, cols].T
        g_ref[cols, :] = cotangent_ref[:, cols].T
        sg_ref[cols, :] = (cotangent_ref[:, cols].astype(f32) * gain_ref[:, cols]).T


def sums_kernel(mixed_ref, res_ref, q_ref, sg_ref, out_ref):
    width, tokens = res_ref.shape
    summed = res_ref[...].astype(f32) + q_ref[...].astype(f32) * mixed_ref[...].astype(f32)
    out_ref[0:1, :] = jnp.sum(summed * summed, axis=0, keepdims=True)
    out_ref[1:2, :] = jnp.sum(sg_ref[...] * summed, axis=0, keepdims=True)


def norm_terms(sums_ref, total):
    inv_rms = lax.rsqrt(sums_ref[0:1, :] * (1.0 / total) + epsilon)
    alpha = inv_rms * inv_rms * inv_rms * sums_ref[1:2, :] * (1.0 / total)
    return inv_rms, alpha


def grad_kernel(total, sums_ref, mixed_ref, res_ref, q_ref, g_ref, sg_ref, out_ref):
    width, tokens = res_ref.shape
    peers, rows, _ = out_ref.shape
    channels = rows // 2
    inv_rms, alpha = norm_terms(sums_ref, total)
    lane = lax.broadcasted_iota(jnp.int32, (tokens, tokens), 1)
    group = tokens // channels
    for j in range(width // tokens):
        cols = pl.ds(j * tokens, tokens)
        dest = pl.ds(j * group, group)
        query = q_ref[cols, :].astype(f32)
        summed = res_ref[cols, :].astype(f32) + query * mixed_ref[cols, :].astype(f32)
        grad_summed = inv_rms * sg_ref[cols, :] - summed * alpha
        out_ref[dest, :channels, :] = (
            (grad_summed * query).astype(bf16).reshape(group, channels, tokens)
        )
        part = g_ref[cols, :].astype(f32) * (summed * inv_rms)
        part = jnp.sum(part, axis=1, keepdims=True)
        ph = part.astype(bf16).astype(f32)
        part = jnp.where(lane < tokens // 2, ph, part - ph).astype(bf16)
        out_ref[dest, channels:, :] = part.reshape(group, channels, tokens)


def norm_kernel(
    total, sums_ref, mixed_ref, res_ref, q_ref, sg_ref, gain_ref, normed_ref, gres_ref, gq_ref
):
    width, tokens = res_ref.shape
    inv_rms, alpha = norm_terms(sums_ref, total)
    for j in range(width // tokens):
        cols = pl.ds(j * tokens, tokens)
        mixed = mixed_ref[cols, :].astype(f32)
        summed = res_ref[cols, :].astype(f32) + q_ref[cols, :].astype(f32) * mixed
        grad_summed = inv_rms * sg_ref[cols, :] - summed * alpha
        normed_ref[:, cols] = ((summed * inv_rms).T * gain_ref[:, cols]).astype(bf16)
        gres_ref[:, cols] = grad_summed.astype(bf16).T
        gq_ref[:, cols] = (grad_summed * mixed).astype(bf16).T


def finish_kernel(recv_ref, key_ref, value_ref, gk_ref, gv_ref, gf_ref, sums_ref):
    tokens, width = key_ref.shape
    peers, rows, _ = recv_ref.shape
    channels = rows // 3
    group = tokens // channels
    quarter = tokens // 4
    for j in range(width // tokens):
        cols = pl.ds(j * tokens, tokens)
        dest = pl.ds(j * group, group)
        back = recv_ref[dest, :channels, :].reshape(tokens, tokens).T.astype(f32)
        gk_ref[:, cols] = (back * value_ref[:, cols].astype(f32)).astype(bf16)
        gv_ref[:, cols] = (back * key_ref[:, cols].astype(f32)).astype(bf16)
        gf_ref[:, cols] = (
            recv_ref[dest, channels : 2 * channels, :].reshape(tokens, tokens).T.astype(f32)
        )
        aux = recv_ref[dest, 2 * channels :, :].reshape(tokens, tokens).T.astype(f32)
        sums_ref[0:1, cols] = aux[0:1] + aux[quarter : quarter + 1]
        sums_ref[1:2, cols] = aux[2 * quarter : 2 * quarter + 1] + aux[3 * quarter : 3 * quarter + 1]


def call(kernel, out_shape, scratch=(), cost=None, smem=None, n_in=0):
    in_specs = [
        pl.BlockSpec(memory_space=pltpu.SMEM if i == smem else pltpu.VMEM) for i in range(n_in)
    ]
    return pl.pallas_call(
        kernel,
        out_shape=out_shape,
        in_specs=in_specs,
        out_specs=jax.tree.map(lambda _: pl.BlockSpec(memory_space=pltpu.VMEM), out_shape),
        scratch_shapes=list(scratch),
        compiler_params=pltpu.CompilerParams(vmem_limit_bytes=48 * 1024 * 1024),
        cost_estimate=cost,
    )


def shape(dims, dtype):
    return jax.ShapeDtypeStruct(dims, dtype)


def on_device(
    residual, query_feats, key_feats, value_feats, filters, cotangent, skip_bias, norm_gain
):
    tokens, width = residual.shape
    peers = lax.axis_size("seq")
    total = float(width * lax.axis_size("chan"))
    channels = width // peers
    constants = [jnp.asarray(t) for t in tables(peers, tokens)]
    half = channels * peers
    vm = pltpu.VMEM

    def exchange(values):
        return lax.all_to_all(values, "seq", split_axis=0, concat_axis=0, tiled=True)

    sent = call(send_kernel, shape((peers, 2 * channels, tokens), bf16), n_in=3)(
        key_feats, value_feats, filters
    )
    received = exchange(sent)
    gain_row = norm_gain[None, :]
    turned = (width, tokens)
    res_t, q_t, g_t, sg_t = call(
        turn_kernel,
        (shape(turned, bf16), shape(turned, bf16), shape(turned, bf16), shape(turned, f32)),
        n_in=4,
        cost=pl.CostEstimate(flops=10**6, bytes_accessed=4 * 10**6, transcendentals=0),
    )(residual, query_feats, cotangent, gain_row)
    skip_here = lax.dynamic_slice_in_dim(skip_bias, lax.axis_index("seq") * channels, channels)
    mixed_sent, spectra = call(
        conv_kernel,
        (shape((peers, channels, tokens), bf16), shape((2 * half, 2 * tokens), f32)),
        scratch=(
            vm((2 * half, tokens), f32),
            vm((2 * half, 2 * tokens), bf16),
            vm((2 * half, 2 * tokens), bf16),
            vm((half, 2 * tokens), f32),
            vm((half, tokens), f32),
        ),
        smem=1,
        n_in=9,
    )(received, skip_here, *constants)
    mixed_t = exchange(mixed_sent).reshape(width, tokens)
    sums = call(sums_kernel, shape((2, tokens), f32), n_in=4)(mixed_t, res_t, q_t, sg_t)
    sums = lax.psum(sums, "chan")
    grad_sent = call(
        functools.partial(grad_kernel, total), shape((peers, 2 * channels, tokens), bf16), n_in=6
    )(sums, mixed_t, res_t, q_t, g_t, sg_t)
    grad_received = exchange(grad_sent)
    plain = (tokens, width)
    normed, grad_residual, grad_query = call(
        functools.partial(norm_kernel, total),
        (shape(plain, bf16), shape(plain, bf16), shape(plain, bf16)),
        n_in=6,
        cost=pl.CostEstimate(flops=10**6, bytes_accessed=4 * 10**6, transcendentals=0),
    )(sums, mixed_t, res_t, q_t, sg_t, gain_row)
    lag_sent = call(
        lag_kernel,
        shape((peers, 3 * channels, tokens), bf16),
        scratch=(
            vm((half, tokens), f32),
            vm((half, 2 * tokens), f32),
            vm((2 * half, 2 * tokens), bf16),
            vm((2 * half, 2 * tokens), bf16),
            vm((2 * half, 2 * tokens), f32),
            vm((2 * half, tokens), f32),
        ),
        n_in=9,
    )(grad_received, spectra, *constants)
    lag_received = exchange(lag_sent)
    grad_key, grad_value, grad_filter, ends = call(
        finish_kernel,
        (shape(plain, bf16), shape(plain, bf16), shape(plain, f32), shape((2, width), f32)),
        n_in=3,
    )(lag_received, key_feats, value_feats)
    return (
        normed,
        grad_residual,
        grad_query,
        grad_key,
        grad_value,
        grad_filter,
        ends[0],
        ends[1],
    )


def solution(mesh):
    return jax.shard_map(
        on_device,
        mesh=mesh,
        in_specs=(P("seq", "chan"),) * 6 + (P("chan"),) * 2,
        out_specs=(P("seq", "chan"),) * 6 + (P("chan"),) * 2,
        check_vma=False,
    )
```

```python
import functools
import math

import jax
import jax.numpy as jnp
import ml_dtypes
import numpy as np
from jax import lax
from jax.experimental import pallas as pl
from jax.experimental.pallas import tpu as pltpu
from jax.sharding import PartitionSpec as P

epsilon = 1e-06
f32 = jnp.float32
bf16 = jnp.bfloat16


def split_host(table):
    high = table.astype(ml_dtypes.bfloat16)
    low = (table - high.astype(np.float64)).astype(ml_dtypes.bfloat16)
    return high, low


@functools.cache
def tables(blocks, lanes):
    length = 2 * blocks * lanes
    k1 = np.arange(blocks)[:, None] + 0.5
    a = np.arange(blocks)[None, :]
    angle = 2.0 * np.pi * k1 * a / (2 * blocks)
    outer = np.concatenate((np.cos(angle), -np.sin(angle)), 0)
    outer_high, outer_low = split_host(outer)
    first = np.concatenate((outer_high, outer_low), 1)
    back = outer.T * (2.0 / length)
    back_high, back_low = split_host(back)
    last = np.concatenate((back_high, back_low, back_high), 1)
    b = np.arange(lanes)[None, :]
    angle = 2.0 * np.pi * k1 * b / length
    twiddle = np.concatenate((np.cos(angle), np.sin(angle)), 0).astype(np.float32)
    angle = 2.0 * np.pi * (np.arange(lanes)[:, None] * b % lanes) / lanes
    cosine, sine = np.cos(angle), np.sin(angle)
    inner = np.block([[cosine, -sine], [sine, cosine]])
    inner_high, inner_low = split_host(inner)
    inner = np.concatenate((inner_high, inner_high, inner_low), 0)
    inverse_high, inverse_low = inner_high.T, inner_low.T
    inverse = np.concatenate((inverse_high, inverse_high, inverse_low), 0)
    return (first, last, twiddle, inner, inverse)


def split(values):
    high = values.astype(bf16)
    low = (values - high.astype(f32)).astype(bf16)
    return high, low


def matmul(left, right):
    return jnp.dot(left, right, preferred_element_type=f32)


def put(u_ref, here, offset, values):
    high, low = split(values)
    width = u_ref.shape[1] // 2
    lanes = values.shape[1]
    u_ref[here, offset : offset + lanes] = high
    u_ref[here, width + offset : width + offset + lanes] = low


def forward(series_ref, stride, rows, first_ref, twiddle_ref, inner_ref, u_ref, out_ref, copies=()):
    blocks = first_ref.shape[0] // 2
    lanes = twiddle_ref.shape[1]
    cosine = twiddle_ref[:blocks]
    sine = twiddle_ref[blocks:]
    for pair in range(rows // 2):
        columns = []
        for row in (2 * pair, 2 * pair + 1):
            x = series_ref[pl.ds(row, blocks, stride=stride), :].astype(bf16)
            columns.append(jnp.concatenate((x, x), 0))
        out = matmul(first_ref[...], jnp.concatenate(columns, 1))
        for i in range(2):
            re = out[:blocks, i * lanes : (i + 1) * lanes]
            im = out[blocks:, i * lanes : (i + 1) * lanes]
            here = pl.ds((2 * pair + i) * blocks, blocks)
            put(u_ref, here, 0, re * cosine + im * sine)
            put(u_ref, here, lanes, im * cosine - re * sine)
    n = 2 * lanes
    chunk = 4 * blocks
    for i in range(rows // 4):
        c = pl.ds(i * chunk, chunk)
        out_ref[c] = matmul(u_ref[c, : 2 * n], inner_ref[: 2 * n]) + matmul(
            u_ref[c, :n], inner_ref[2 * n :]
        )
        if copies:
            copies[i].start()


def inverse(rows, last_ref, twiddle_ref, inverse_ref, u_ref, z_ref, out_ref, stride):
    blocks = last_ref.shape[0]
    lanes = twiddle_ref.shape[1]
    cosine = twiddle_ref[:blocks]
    sine = twiddle_ref[blocks:]
    n = 2 * lanes
    chunk = 4 * blocks
    for i in range(rows // 4):
        c = pl.ds(i * chunk, chunk)
        z_ref[c] = matmul(u_ref[c, : 2 * n], inverse_ref[: 2 * n]) + matmul(
            u_ref[c, :n], inverse_ref[2 * n :]
        )
    for pair in range(rows // 2):
        columns = []
        for row in (2 * pair, 2 * pair + 1):
            re = z_ref[pl.ds(row * blocks, blocks), :lanes]
            im = z_ref[pl.ds(row * blocks, blocks), lanes:]
            zh, zl = split(
                jnp.concatenate((re * cosine - im * sine, im * cosine + re * sine), 0)
            )
            columns.append(jnp.concatenate((zh, zh, zl), 0))
        out = matmul(last_ref[...], jnp.concatenate(columns, 1))
        for i in range(2):
            out_ref[pl.ds(2 * pair + i, blocks, stride=stride), :] = out[
                :, i * lanes : (i + 1) * lanes
            ]


def copies_of(source_ref, target_ref, sems):
    count = sems.shape[0]
    chunk = source_ref.shape[0] // count
    return [
        pltpu.make_async_copy(
            source_ref.at[pl.ds(i * chunk, chunk)],
            target_ref.at[pl.ds(i * chunk, chunk)],
            sems.at[i],
        )
        for i in range(count)
    ]


def conv_kernel(
    recv_ref, skip_ref, first_ref, last_ref, twiddle_ref, inner_ref, inverse_ref,
    mixed_ref, kept_ref, spec_ref, x_ref, u_ref, z_ref, y_ref, sems,
):
    blocks, rows, lanes = recv_ref.shape
    channels = rows // 2
    half = channels * blocks
    wide = rows + 8
    for a in range(blocks):
        x_ref[pl.ds(a * wide, rows), :] = recv_ref[a].astype(f32)
    copies = copies_of(spec_ref, kept_ref, sems)
    forward(x_ref, wide, rows, first_ref, twiddle_ref, inner_ref, u_ref, spec_ref, copies)
    for c in range(channels):
        prod = pl.ds(c * blocks, blocks)
        filt = pl.ds(half + c * blocks, blocks)
        fre = spec_ref[filt, :lanes] + skip_ref[c]
        fim = spec_ref[filt, lanes:]
        pre, pim = spec_ref[prod, :lanes], spec_ref[prod, lanes:]
        put(u_ref, prod, 0, pre * fre - pim * fim)
        put(u_ref, prod, lanes, pre * fim + pim * fre)
    wide = channels + 8
    inverse(channels, last_ref, twiddle_ref, inverse_ref, u_ref, z_ref, y_ref, wide)
    for a in range(blocks):
        mixed_ref[a] = y_ref[pl.ds(a * wide, channels), :].astype(bf16)
    for copy in copies:
        copy.wait()


def lag_kernel(
    recv_ref, skip_ref, first_ref, last_ref, twiddle_ref, inner_ref, inverse_ref, kept_ref, *rest
):
    out_ref, spec_ref, x_ref, g_ref, u_ref, z_ref, y_ref, sems = rest[-8:]
    blocks, channels, lanes = recv_ref.shape
    rows = 2 * channels
    half = channels * blocks
    copies = copies_of(kept_ref, spec_ref, sems)
    ahead = len(copies) // 2
    for i in range(ahead):
        copies[i].start()
        copies[ahead + i].start()
    wide = channels + 8
    for a in range(blocks):
        x_ref[pl.ds(a * wide, channels), :] = recv_ref[a].astype(f32)
    forward(x_ref, wide, channels, first_ref, twiddle_ref, inner_ref, u_ref, g_ref)
    for c in range(channels):
        if c % (channels // ahead) == 0:
            copies[c * ahead // channels].wait()
            copies[ahead + c * ahead // channels].wait()
        prod = pl.ds(c * blocks, blocks)
        filt = pl.ds(half + c * blocks, blocks)
        gre, gim = g_ref[prod, :lanes], g_ref[prod, lanes:]
        for source, target in ((filt, prod), (prod, filt)):
            sre, sim = spec_ref[source, :lanes], spec_ref[source, lanes:]
            if source is filt:
                sre = sre + skip_ref[c]
            put(u_ref, target, 0, sre * gre + sim * gim)
            put(u_ref, target, lanes, sre * gim - sim * gre)
    wide = rows + 8
    inverse(rows, last_ref, twiddle_ref, inverse_ref, u_ref, z_ref, y_ref, wide)
    for a in range(blocks):
        out_ref[a] = y_ref[pl.ds(a * wide, rows), :].astype(bf16)


def send_kernel(
    key_hbm, value_hbm, filters_hbm, out_ref, key_ref, value_ref, filters_ref, sems
):
    tokens, width = key_ref.shape
    peers, rows, _ = out_ref.shape
    channels = rows // 2
    group = tokens // channels
    copies = [
        pltpu.make_async_copy(source, target, sems.at[i])
        for i, (source, target) in enumerate(
            ((filters_hbm, filters_ref), (key_hbm, key_ref), (value_hbm, value_ref))
        )
    ]
    for copy in copies:
        copy.start()
    copies[0].wait()
    for j in range(width // tokens):
        cols = pl.ds(j * tokens, tokens)
        dest = pl.ds(j * group, group)
        out_ref[dest, channels:, :] = filters_ref[:, cols].T.reshape(group, channels, tokens)
    copies[1].wait()
    copies[2].wait()
    for j in range(width // tokens):
        cols = pl.ds(j * tokens, tokens)
        dest = pl.ds(j * group, group)
        product = key_ref[:, cols].astype(f32) * value_ref[:, cols].astype(f32)
        out_ref[dest, :channels, :] = product.astype(bf16).T.reshape(group, channels, tokens)


def turn_kernel(residual_ref, query_ref, cotangent_ref, gain_ref, res_ref, q_ref, sg_ref):
    tokens, width = residual_ref.shape
    for j in range(width // tokens):
        cols = pl.ds(j * tokens, tokens)
        res_ref[cols, :] = residual_ref[:, cols].T
        q_ref[cols, :] = query_ref[:, cols].T
        sg_ref[cols, :] = (cotangent_ref[:, cols].astype(f32) * gain_ref[:, cols]).T


def sums_kernel(mixed_ref, res_ref, q_ref, sg_ref, out_ref):
    width, tokens = res_ref.shape
    summed = res_ref[...].astype(f32) + q_ref[...].astype(f32) * mixed_ref[...].astype(f32)
    out_ref[0:1, :] = jnp.sum(summed * summed, axis=0, keepdims=True)
    out_ref[1:2, :] = jnp.sum(sg_ref[...] * summed, axis=0, keepdims=True)


def norm_terms(sums_refs, total):
    near, far = sums_refs
    sums = (near[...] + far[...]) * (1.0 / total)
    inv_rms = lax.rsqrt(sums[0:1, :] + epsilon)
    alpha = inv_rms * inv_rms * inv_rms * sums[1:2, :]
    return inv_rms, alpha


def grad_kernel(total, near_ref, far_ref, mixed_ref, res_ref, q_ref, sg_ref, out_ref):
    inv_rms, alpha = norm_terms((near_ref, far_ref), total)
    query = q_ref[...].astype(f32)
    summed = res_ref[...].astype(f32) + query * mixed_ref[...].astype(f32)
    grad_summed = inv_rms * sg_ref[...] - summed * alpha
    out_ref[...] = (grad_summed * query).astype(bf16)


def norm_kernel(
    total, near_ref, far_ref, mixed_ref, res_ref, q_ref, sg_ref, gain_ref, cotangent_ref, key_ref, value_ref,
    normed_ref, gres_ref, gq_ref, ends_ref,
):
    width, tokens = res_ref.shape
    inv_rms, alpha = norm_terms((near_ref, far_ref), total)
    for j in range(width // tokens):
        cols = pl.ds(j * tokens, tokens)
        mixed = mixed_ref[cols, :].astype(f32)
        query = q_ref[cols, :].astype(f32)
        summed = res_ref[cols, :].astype(f32) + query * mixed
        grad_summed = inv_rms * sg_ref[cols, :] - summed * alpha
        unit = (summed * inv_rms).T
        normed_ref[:, cols] = (unit * gain_ref[:, cols]).astype(bf16)
        gres_ref[:, cols] = grad_summed.astype(bf16).T
        gq_ref[:, cols] = (grad_summed * mixed).astype(bf16).T
        grad_mixed = (grad_summed * query).astype(bf16).T.astype(f32)
        product = key_ref[:, cols].astype(f32) * value_ref[:, cols].astype(f32)
        product = product.astype(bf16).astype(f32)
        ends_ref[0:1, cols] = jnp.sum(grad_mixed * product, axis=0, keepdims=True)
        ends_ref[1:2, cols] = jnp.sum(
            cotangent_ref[:, cols].astype(f32) * unit, axis=0, keepdims=True
        )


def finish_kernel(recv_ref, key_ref, value_ref, gk_ref, gv_ref, gf_ref):
    tokens, width = key_ref.shape
    peers, rows, _ = recv_ref.shape
    channels = rows // 2
    group = tokens // channels
    for j in range(width // tokens):
        cols = pl.ds(j * tokens, tokens)
        dest = pl.ds(j * group, group)
        back = recv_ref[dest, :channels, :].reshape(tokens, tokens).T.astype(f32)
        gk_ref[:, cols] = (back * value_ref[:, cols].astype(f32)).astype(bf16)
        gv_ref[:, cols] = (back * key_ref[:, cols].astype(f32)).astype(bf16)
        gf_ref[:, cols] = recv_ref[dest, channels:, :].reshape(tokens, tokens).T.astype(f32)


def places(side, stride, count, step):
    pairs = []
    for source in range(count):
        place = source // stride % side
        pairs.append((source, source + ((place + step) % side - place) * stride))
    return pairs


def sum_over(values, axis, side, stride):
    count = lax.axis_size(axis)
    moved = [
        lax.ppermute(values, axis, places(side, stride, count, step)) for step in range(1, side)
    ]
    for part in moved:
        values = values + part
    return values


def call(kernel, out_shape, n_in, scratch=(), cost=None, smem=(), hbm=(), hbm_out=()):
    def place(i, scalar, far):
        space = pltpu.SMEM if i in scalar else pltpu.HBM if i in far else pltpu.VMEM
        return pl.BlockSpec(memory_space=space)

    outs = out_shape if isinstance(out_shape, tuple) else (out_shape,)
    out_specs = tuple(place(i, (), hbm_out) for i in range(len(outs)))
    return pl.pallas_call(
        kernel,
        out_shape=out_shape,
        in_specs=[place(i, smem, hbm) for i in range(n_in)],
        out_specs=out_specs if isinstance(out_shape, tuple) else out_specs[0],
        scratch_shapes=list(scratch),
        compiler_params=pltpu.CompilerParams(vmem_limit_bytes=48 * 1024 * 1024),
        cost_estimate=cost,
    )


def far_memory(values):
    return pltpu.with_memory_space_constraint(values, pltpu.HBM)


def shape(dims, dtype):
    return jax.ShapeDtypeStruct(dims, dtype)


def run_conv(received, skip_here):
    peers, rows, tokens = received.shape
    channels = rows // 2
    half = channels * peers
    spectra_shape = (2 * half, 2 * tokens)
    vm = pltpu.VMEM
    return call(
        conv_kernel,
        (shape((peers, channels, tokens), bf16), pltpu.HBM(spectra_shape, f32)),
        n_in=7,
        smem=(1,),
        hbm_out=(1,),
        scratch=(
            vm(spectra_shape, f32),
            vm((2 * half + 8 * peers, tokens), f32),
            vm((2 * half, 4 * tokens), bf16),
            vm((half, 2 * tokens), f32),
            vm((half + 8 * peers, tokens), f32),
            pltpu.SemaphoreType.DMA((rows // 4,)),
        ),
    )(received, skip_here, *tables(peers, tokens))


def run_lag(received, skip_here, spectra, *after):
    peers, channels, tokens = received.shape
    half = channels * peers
    spectra_shape = (2 * half, 2 * tokens)
    vm = pltpu.VMEM
    return call(
        lag_kernel,
        shape((peers, 2 * channels, tokens), bf16),
        n_in=8 + len(after),
        smem=(1,),
        hbm=(7, 8),
        scratch=(
            vm(spectra_shape, f32),
            vm((half + 8 * peers, tokens), f32),
            vm((half, 2 * tokens), f32),
            vm((2 * half, 4 * tokens), bf16),
            vm(spectra_shape, f32),
            vm((2 * half + 8 * peers, tokens), f32),
            pltpu.SemaphoreType.DMA((channels // 2,)),
        ),
    )(received, skip_here, *tables(peers, tokens), far_memory(spectra), *after)


sides = (4, 4, 4)


def on_device(
    residual, query_feats, key_feats, value_feats, filters, cotangent, skip_bias, norm_gain
):
    tokens, width = residual.shape
    peers = lax.axis_size("seq")
    total = float(width * lax.axis_size("chan"))
    channels = width // peers
    vm = pltpu.VMEM

    def exchange(values):
        return lax.all_to_all(values, "seq", split_axis=0, concat_axis=0, tiled=True)

    plain = (tokens, width)
    turned = (width, tokens)
    dma = pltpu.SemaphoreType.DMA
    aside = pl.CostEstimate(flops=10**6, bytes_accessed=4 * 10**6, transcendentals=0)
    sent = call(
        send_kernel,
        shape((peers, 2 * channels, tokens), bf16),
        n_in=3,
        hbm=(0, 1, 2),
        scratch=(vm(plain, bf16), vm(plain, bf16), vm(plain, bf16), dma((3,))),
    )(far_memory(key_feats), far_memory(value_feats), far_memory(filters))
    received = exchange(sent)
    gain_row = norm_gain[None, :]
    res_t, q_t, sg_t = call(
        turn_kernel,
        (shape(turned, bf16), shape(turned, bf16), shape(turned, f32)),
        n_in=4,
        cost=aside,
    )(residual, query_feats, cotangent, gain_row)
    skip_here = lax.dynamic_slice_in_dim(skip_bias, lax.axis_index("seq") * channels, channels)
    mixed_sent, spectra = run_conv(received, skip_here)
    mixed_t = exchange(mixed_sent).reshape(width, tokens)
    sums = call(sums_kernel, shape((2, tokens), f32), n_in=4)(mixed_t, res_t, q_t, sg_t)
    near = sum_over(sums, "chan", 2, 1)
    far = lax.ppermute(near, "chan", places(2, 2, 4, 1))
    grad_sent = call(
        functools.partial(grad_kernel, total), shape(turned, bf16), n_in=6
    )(near, far, mixed_t, res_t, q_t, sg_t)
    grad_received = exchange(grad_sent.reshape(peers, channels, tokens))
    normed, grad_residual, grad_query, ends = call(
        functools.partial(norm_kernel, total),
        (shape(plain, bf16), shape(plain, bf16), shape(plain, bf16), shape((2, width), f32)),
        n_in=10,
        cost=aside,
    )(near, far, mixed_t, res_t, q_t, sg_t, gain_row, cotangent, key_feats, value_feats)
    side_z, side_y, side_x = sides
    ends = sum_over(ends, "seq", side_x, 1)
    lag_sent = run_lag(grad_received, skip_here, spectra, ends)
    ends = sum_over(ends, "seq", side_y, side_x)
    ends = sum_over(ends, "seq", side_z, side_x * side_y)
    lag_received = exchange(lag_sent)
    grad_key, grad_value, grad_filter = call(
        finish_kernel,
        (shape(plain, bf16), shape(plain, bf16), shape(plain, f32)),
        n_in=3,
    )(lag_received, key_feats, value_feats)
    return (
        normed,
        grad_residual,
        grad_query,
        grad_key,
        grad_value,
        grad_filter,
        ends[0],
        ends[1],
    )


def solution(mesh):
    return jax.shard_map(
        on_device,
        mesh=mesh,
        in_specs=(P("seq", "chan"),) * 6 + (P("chan"),) * 2,
        out_specs=(P("seq", "chan"),) * 6 + (P("chan"),) * 2,
        check_vma=False,
    )
```

```python
import functools
import math

import jax
import jax.numpy as jnp
import ml_dtypes
import numpy as np
from jax import lax
from jax.experimental import pallas as pl
from jax.experimental.pallas import tpu as pltpu
from jax.sharding import PartitionSpec as P

epsilon = 1e-06
f32 = jnp.float32
bf16 = jnp.bfloat16


def split_host(table):
    high = table.astype(ml_dtypes.bfloat16)
    low = (table - high.astype(np.float64)).astype(ml_dtypes.bfloat16)
    return high, low


@functools.cache
def tables(blocks, lanes):
    length = 2 * blocks * lanes
    k1 = np.arange(blocks)[:, None] + 0.5
    a = np.arange(blocks)[None, :]
    angle = 2.0 * np.pi * k1 * a / (2 * blocks)
    outer = np.concatenate((np.cos(angle), -np.sin(angle)), 0)
    outer_high, outer_low = split_host(outer)
    first = np.concatenate((outer_high, outer_low), 1)
    back = outer.T * (2.0 / length)
    back_high, back_low = split_host(back)
    last = np.concatenate((back_high, back_low, back_high), 1)
    b = np.arange(lanes)[None, :]
    angle = 2.0 * np.pi * k1 * b / length
    twiddle = np.concatenate((np.cos(angle), np.sin(angle)), 0).astype(np.float32)
    angle = 2.0 * np.pi * (np.arange(lanes)[:, None] * b % lanes) / lanes
    cosine, sine = np.cos(angle), np.sin(angle)
    inner = np.block([[cosine, -sine], [sine, cosine]])
    inner_high, inner_low = split_host(inner)
    inner = np.concatenate((inner_high, inner_high, inner_low), 0)
    inverse_high, inverse_low = inner_high.T, inner_low.T
    inverse = np.concatenate((inverse_high, inverse_high, inverse_low), 0)
    return (first, last, twiddle, inner, inverse)


def split(values):
    high = values.astype(bf16)
    low = (values - high.astype(f32)).astype(bf16)
    return high, low


def matmul(left, right):
    return jnp.dot(left, right, preferred_element_type=f32)


def put(u_ref, here, offset, values):
    high, low = split(values)
    width = u_ref.shape[1] // 2
    lanes = values.shape[1]
    u_ref[here, offset : offset + lanes] = high
    u_ref[here, width + offset : width + offset + lanes] = low


def forward(series_ref, stride, rows, first_ref, twiddle_ref, inner_ref, u_ref, out_ref, copies=()):
    blocks = first_ref.shape[0] // 2
    lanes = twiddle_ref.shape[1]
    cosine = twiddle_ref[:blocks]
    sine = twiddle_ref[blocks:]
    for pair in range(rows // 2):
        columns = []
        for row in (2 * pair, 2 * pair + 1):
            x = series_ref[pl.ds(row, blocks, stride=stride), :].astype(bf16)
            columns.append(jnp.concatenate((x, x), 0))
        out = matmul(first_ref[...], jnp.concatenate(columns, 1))
        for i in range(2):
            re = out[:blocks, i * lanes : (i + 1) * lanes]
            im = out[blocks:, i * lanes : (i + 1) * lanes]
            here = pl.ds((2 * pair + i) * blocks, blocks)
            put(u_ref, here, 0, re * cosine + im * sine)
            put(u_ref, here, lanes, im * cosine - re * sine)
    n = 2 * lanes
    chunk = 4 * blocks
    for i in range(rows // 4):
        c = pl.ds(i * chunk, chunk)
        out_ref[c] = matmul(u_ref[c, : 2 * n], inner_ref[: 2 * n]) + matmul(
            u_ref[c, :n], inner_ref[2 * n :]
        )
        if copies:
            copies[i].start()


def inverse(rows, last_ref, twiddle_ref, inverse_ref, u_ref, z_ref, out_ref, stride, base=0):
    blocks = last_ref.shape[0]
    lanes = twiddle_ref.shape[1]
    cosine = twiddle_ref[:blocks]
    sine = twiddle_ref[blocks:]
    n = 2 * lanes
    chunk = 4 * blocks
    for i in range(rows // 4):
        c = pl.ds(base * blocks + i * chunk, chunk)
        z_ref[c] = matmul(u_ref[c, : 2 * n], inverse_ref[: 2 * n]) + matmul(
            u_ref[c, :n], inverse_ref[2 * n :]
        )
    for pair in range(rows // 2):
        columns = []
        for row in (2 * pair, 2 * pair + 1):
            re = z_ref[pl.ds((base + row) * blocks, blocks), :lanes]
            im = z_ref[pl.ds((base + row) * blocks, blocks), lanes:]
            zh, zl = split(
                jnp.concatenate((re * cosine - im * sine, im * cosine + re * sine), 0)
            )
            columns.append(jnp.concatenate((zh, zh, zl), 0))
        out = matmul(last_ref[...], jnp.concatenate(columns, 1))
        for i in range(2):
            out_ref[pl.ds(base + 2 * pair + i, blocks, stride=stride), :] = out[
                :, i * lanes : (i + 1) * lanes
            ]


def copies_of(source_ref, target_ref, sems):
    count = sems.shape[0]
    chunk = source_ref.shape[0] // count
    return [
        pltpu.make_async_copy(
            source_ref.at[pl.ds(i * chunk, chunk)],
            target_ref.at[pl.ds(i * chunk, chunk)],
            sems.at[i],
        )
        for i in range(count)
    ]


def conv_kernel(
    recv_ref, skip_ref, first_ref, last_ref, twiddle_ref, inner_ref, inverse_ref,
    mixed_ref, kept_ref, spec_ref, x_ref, u_ref, z_ref, y_ref, sems,
):
    blocks, rows, lanes = recv_ref.shape
    channels = rows // 2
    half = channels * blocks
    wide = rows + 8
    for a in range(blocks):
        x_ref[pl.ds(a * wide, rows), :] = recv_ref[a].astype(f32)
    copies = copies_of(spec_ref, kept_ref, sems)
    forward(x_ref, wide, rows, first_ref, twiddle_ref, inner_ref, u_ref, spec_ref, copies)
    for c in range(channels):
        prod = pl.ds(c * blocks, blocks)
        filt = pl.ds(half + c * blocks, blocks)
        fre = spec_ref[filt, :lanes] + skip_ref[c]
        fim = spec_ref[filt, lanes:]
        pre, pim = spec_ref[prod, :lanes], spec_ref[prod, lanes:]
        put(u_ref, prod, 0, pre * fre - pim * fim)
        put(u_ref, prod, lanes, pre * fim + pim * fre)
    wide = channels + 8
    inverse(channels, last_ref, twiddle_ref, inverse_ref, u_ref, z_ref, y_ref, wide)
    for a in range(blocks):
        mixed_ref[a] = y_ref[pl.ds(a * wide, channels), :].astype(bf16)
    for copy in copies:
        copy.wait()


def lag_kernel(
    recv_ref, skip_ref, first_ref, last_ref, twiddle_ref, inner_ref, inverse_ref, kept_ref, *rest
):
    out_ref, spec_ref, x_ref, g_ref, u_ref, z_ref, y_ref, ready_ref, sems, out_sems = rest[-10:]
    blocks, channels, lanes = recv_ref.shape
    rows = 2 * channels
    half = channels * blocks
    copies = copies_of(kept_ref, spec_ref, sems)
    ahead = len(copies) // 2
    for i in range(ahead):
        copies[ahead + i].start()
    for i in range(ahead):
        copies[i].start()
    wide = channels + 8
    for a in range(blocks):
        x_ref[pl.ds(a * wide, channels), :] = recv_ref[a].astype(f32)
    forward(x_ref, wide, channels, first_ref, twiddle_ref, inner_ref, u_ref, g_ref)
    wide = rows + 8
    leaving = []
    for source, target, lead in ((half, 0, ahead), (0, half, 0)):
        for c in range(channels):
            if c % (channels // ahead) == 0:
                copies[lead + c * ahead // channels].wait()
            grad = pl.ds(c * blocks, blocks)
            gre, gim = g_ref[grad, :lanes], g_ref[grad, lanes:]
            here = pl.ds(source + c * blocks, blocks)
            sre, sim = spec_ref[here, :lanes], spec_ref[here, lanes:]
            if source:
                sre = sre + skip_ref[c]
            put(u_ref, pl.ds(target + c * blocks, blocks), 0, sre * gre + sim * gim)
            put(u_ref, pl.ds(target + c * blocks, blocks), lanes, sre * gim - sim * gre)
        inverse(
            channels, last_ref, twiddle_ref, inverse_ref, u_ref, z_ref, y_ref, wide, target // blocks
        )
        first = target // blocks
        for a in range(blocks):
            ready_ref[first // channels, a] = y_ref[pl.ds(a * wide + first, channels), :].astype(bf16)
        leaving.append(
            pltpu.make_async_copy(
                ready_ref.at[first // channels],
                out_ref.at[:, pl.ds(first, channels), :],
                out_sems.at[first // channels],
            )
        )
        leaving[-1].start()
    for copy in leaving:
        copy.wait()


def send_kernel(
    key_hbm, value_hbm, filters_hbm, out_hbm, key_ref, value_ref, filters_ref, out_ref, sems, out_sems
):
    tokens, width = key_ref.shape
    peers, rows, _ = out_ref.shape
    channels = rows // 2
    group = tokens // channels
    parts = out_sems.shape[0]
    arriving = []
    for part in range(parts):
        cols = pl.ds(part * (width // parts), width // parts)
        pairs = ((key_hbm, key_ref), (value_hbm, value_ref), (filters_hbm, filters_ref))
        arriving.append(
            [
                pltpu.make_async_copy(source.at[:, cols], target.at[:, cols], sems.at[part, i])
                for i, (source, target) in enumerate(pairs)
            ]
        )
        for copy in arriving[-1]:
            copy.start()
    leaving = []
    for part in range(parts):
        for copy in arriving[part]:
            copy.wait()
        steps = width // tokens // parts
        for j in range(part * steps, (part + 1) * steps):
            cols = pl.ds(j * tokens, tokens)
            dest = pl.ds(j * group, group)
            product = key_ref[:, cols].astype(f32) * value_ref[:, cols].astype(f32)
            out_ref[dest, :channels, :] = product.astype(bf16).T.reshape(group, channels, tokens)
            out_ref[dest, channels:, :] = filters_ref[:, cols].T.reshape(group, channels, tokens)
        dest = pl.ds(part * (peers // parts), peers // parts)
        leaving.append(
            pltpu.make_async_copy(out_ref.at[dest], out_hbm.at[dest], out_sems.at[part])
        )
        leaving[-1].start()
    for copy in leaving:
        copy.wait()


def turn_kernel(residual_ref, query_ref, cotangent_ref, gain_ref, res_ref, q_ref, sg_ref):
    tokens, width = residual_ref.shape
    for j in range(width // tokens):
        cols = pl.ds(j * tokens, tokens)
        res_ref[cols, :] = residual_ref[:, cols].T
        q_ref[cols, :] = query_ref[:, cols].T
        sg_ref[cols, :] = (cotangent_ref[:, cols].astype(f32) * gain_ref[:, cols]).T


def sums_kernel(mixed_ref, res_ref, q_ref, sg_ref, out_ref):
    width, tokens = res_ref.shape
    summed = res_ref[...].astype(f32) + q_ref[...].astype(f32) * mixed_ref[...].astype(f32)
    out_ref[0:1, :] = jnp.sum(summed * summed, axis=0, keepdims=True)
    out_ref[1:2, :] = jnp.sum(sg_ref[...] * summed, axis=0, keepdims=True)


def norm_terms(sums_refs, total):
    near, far = sums_refs
    sums = (near[...] + far[...]) * (1.0 / total)
    inv_rms = lax.rsqrt(sums[0:1, :] + epsilon)
    alpha = inv_rms * inv_rms * inv_rms * sums[1:2, :]
    return inv_rms, alpha


def grad_kernel(total, near_ref, far_ref, mixed_ref, res_ref, q_ref, sg_ref, out_hbm, out_ref, sems):
    inv_rms, alpha = norm_terms((near_ref, far_ref), total)
    parts = sems.shape[0]
    size = res_ref.shape[0] // parts
    leaving = []
    for part in range(parts):
        here = pl.ds(part * size, size)
        query = q_ref[here].astype(f32)
        summed = res_ref[here].astype(f32) + query * mixed_ref[here].astype(f32)
        grad_summed = inv_rms * sg_ref[here] - summed * alpha
        out_ref[here] = (grad_summed * query).astype(bf16)
        leaving.append(
            pltpu.make_async_copy(out_ref.at[here], out_hbm.at[here], sems.at[part])
        )
        leaving[-1].start()
    for copy in leaving:
        copy.wait()


def norm_kernel(
    total, near_ref, far_ref, mixed_ref, res_ref, q_ref, sg_ref, gain_ref, cotangent_ref, key_ref, value_ref,
    normed_ref, gres_ref, gq_ref, ends_ref,
):
    width, tokens = res_ref.shape
    inv_rms, alpha = norm_terms((near_ref, far_ref), total)
    for j in range(width // tokens):
        cols = pl.ds(j * tokens, tokens)
        mixed = mixed_ref[cols, :].astype(f32)
        query = q_ref[cols, :].astype(f32)
        summed = res_ref[cols, :].astype(f32) + query * mixed
        grad_summed = inv_rms * sg_ref[cols, :] - summed * alpha
        unit = (summed * inv_rms).T
        normed_ref[:, cols] = (unit * gain_ref[:, cols]).astype(bf16)
        gres_ref[:, cols] = grad_summed.astype(bf16).T
        gq_ref[:, cols] = (grad_summed * mixed).astype(bf16).T
        grad_mixed = (grad_summed * query).astype(bf16).T.astype(f32)
        product = key_ref[:, cols].astype(f32) * value_ref[:, cols].astype(f32)
        product = product.astype(bf16).astype(f32)
        ends_ref[0:1, cols] = jnp.sum(grad_mixed * product, axis=0, keepdims=True)
        ends_ref[1:2, cols] = jnp.sum(
            cotangent_ref[:, cols].astype(f32) * unit, axis=0, keepdims=True
        )


def finish_kernel(
    recv_ref, key_ref, value_ref, gk_hbm, gv_hbm, gf_hbm, gk_ref, gv_ref, gf_ref, sems
):
    tokens, width = key_ref.shape
    peers, rows, _ = recv_ref.shape
    channels = rows // 2
    group = tokens // channels
    parts = sems.shape[0]
    steps = width // tokens // parts
    leaving = []
    for part in range(parts):
        for j in range(part * steps, (part + 1) * steps):
            cols = pl.ds(j * tokens, tokens)
            dest = pl.ds(j * group, group)
            back = recv_ref[dest, :channels, :].reshape(tokens, tokens).T.astype(f32)
            gk_ref[:, cols] = (back * value_ref[:, cols].astype(f32)).astype(bf16)
            gv_ref[:, cols] = (back * key_ref[:, cols].astype(f32)).astype(bf16)
            gf_ref[:, cols] = recv_ref[dest, channels:, :].reshape(tokens, tokens).T.astype(f32)
        cols = pl.ds(part * (width // parts), width // parts)
        pairs = ((gk_ref, gk_hbm), (gv_ref, gv_hbm), (gf_ref, gf_hbm))
        for i, (source, target) in enumerate(pairs):
            leaving.append(
                pltpu.make_async_copy(source.at[:, cols], target.at[:, cols], sems.at[part, i])
            )
            leaving[-1].start()
    for copy in leaving:
        copy.wait()


def places(side, stride, count, step):
    pairs = []
    for source in range(count):
        place = source // stride % side
        pairs.append((source, source + ((place + step) % side - place) * stride))
    return pairs


def add_kernel(*refs):
    *sources, out_ref = refs
    own, *others = (ref[...] for ref in sources)
    out_ref[...] = sum(others, own)


def sum_over(values, axis, side, stride, cost=None):
    count = lax.axis_size(axis)
    moved = [
        lax.ppermute(values, axis, places(side, stride, count, step)) for step in range(1, side)
    ]
    if cost is not None:
        out = shape(values.shape, values.dtype)
        return call(add_kernel, out, n_in=side, cost=cost)(values, *moved)
    for part in moved:
        values = values + part
    return values


def call(kernel, out_shape, n_in, scratch=(), cost=None, smem=(), hbm=(), hbm_out=()):
    def place(i, scalar, far):
        space = pltpu.SMEM if i in scalar else pltpu.HBM if i in far else pltpu.VMEM
        return pl.BlockSpec(memory_space=space)

    outs = out_shape if isinstance(out_shape, tuple) else (out_shape,)
    out_specs = tuple(place(i, (), hbm_out) for i in range(len(outs)))
    return pl.pallas_call(
        kernel,
        out_shape=out_shape,
        in_specs=[place(i, smem, hbm) for i in range(n_in)],
        out_specs=out_specs if isinstance(out_shape, tuple) else out_specs[0],
        scratch_shapes=list(scratch),
        compiler_params=pltpu.CompilerParams(vmem_limit_bytes=48 * 1024 * 1024),
        cost_estimate=cost,
    )


def far_memory(values):
    return pltpu.with_memory_space_constraint(values, pltpu.HBM)


def shape(dims, dtype):
    return jax.ShapeDtypeStruct(dims, dtype)


def run_conv(received, skip_here):
    peers, rows, tokens = received.shape
    channels = rows // 2
    half = channels * peers
    spectra_shape = (2 * half, 2 * tokens)
    vm = pltpu.VMEM
    return call(
        conv_kernel,
        (shape((peers, channels, tokens), bf16), pltpu.HBM(spectra_shape, f32)),
        n_in=7,
        smem=(1,),
        hbm_out=(1,),
        scratch=(
            vm(spectra_shape, f32),
            vm((2 * half + 8 * peers, tokens), f32),
            vm((2 * half, 4 * tokens), bf16),
            vm((half, 2 * tokens), f32),
            vm((half + 8 * peers, tokens), f32),
            pltpu.SemaphoreType.DMA((rows // 4,)),
        ),
    )(received, skip_here, *tables(peers, tokens))


def run_lag(received, skip_here, spectra, *after):
    peers, channels, tokens = received.shape
    half = channels * peers
    spectra_shape = (2 * half, 2 * tokens)
    vm = pltpu.VMEM
    return call(
        lag_kernel,
        pltpu.HBM((peers, 2 * channels, tokens), bf16),
        n_in=8 + len(after),
        smem=(1,),
        hbm=(7, 8),
        hbm_out=(0,),
        scratch=(
            vm(spectra_shape, f32),
            vm((half + 8 * peers, tokens), f32),
            vm((half, 2 * tokens), f32),
            vm((2 * half, 4 * tokens), bf16),
            vm(spectra_shape, f32),
            vm((2 * half + 8 * peers, tokens), f32),
            vm((2, peers, channels, tokens), bf16),
            pltpu.SemaphoreType.DMA((channels // 2,)),
            pltpu.SemaphoreType.DMA((2,)),
        ),
    )(received, skip_here, *tables(peers, tokens), far_memory(spectra), *after)


sides = (4, 4, 4)


def on_device(
    residual, query_feats, key_feats, value_feats, filters, cotangent, skip_bias, norm_gain
):
    tokens, width = residual.shape
    peers = lax.axis_size("seq")
    total = float(width * lax.axis_size("chan"))
    channels = width // peers
    vm = pltpu.VMEM

    def exchange(values):
        return lax.all_to_all(values, "seq", split_axis=0, concat_axis=0, tiled=True)

    plain = (tokens, width)
    turned = (width, tokens)
    dma = pltpu.SemaphoreType.DMA
    aside = pl.CostEstimate(flops=10**6, bytes_accessed=4 * 10**6, transcendentals=0)
    parts = 4
    sent = call(
        send_kernel,
        pltpu.HBM((peers, 2 * channels, tokens), bf16),
        n_in=3,
        hbm=(0, 1, 2),
        hbm_out=(0,),
        scratch=(
            vm(plain, bf16),
            vm(plain, bf16),
            vm(plain, bf16),
            vm((peers, 2 * channels, tokens), bf16),
            dma((parts, 3)),
            dma((parts,)),
        ),
    )(far_memory(key_feats), far_memory(value_feats), far_memory(filters))
    received = exchange(sent)
    gain_row = norm_gain[None, :]
    res_t, q_t, sg_t = call(
        turn_kernel,
        (shape(turned, bf16), shape(turned, bf16), shape(turned, f32)),
        n_in=4,
        cost=aside,
    )(residual, query_feats, cotangent, gain_row)
    skip_here = lax.dynamic_slice_in_dim(skip_bias, lax.axis_index("seq") * channels, channels)
    mixed_sent, spectra = run_conv(received, skip_here)
    mixed_t = exchange(mixed_sent).reshape(width, tokens)
    sums = call(sums_kernel, shape((2, tokens), f32), n_in=4)(mixed_t, res_t, q_t, sg_t)
    near = sum_over(sums, "chan", 2, 1)
    far = lax.ppermute(near, "chan", places(2, 2, 4, 1))
    grad_sent = call(
        functools.partial(grad_kernel, total),
        pltpu.HBM(turned, bf16),
        n_in=6,
        hbm_out=(0,),
        scratch=(vm(turned, bf16), dma((parts,))),
    )(near, far, mixed_t, res_t, q_t, sg_t)
    grad_received = exchange(grad_sent.reshape(peers, channels, tokens))
    normed, grad_residual, grad_query, ends = call(
        functools.partial(norm_kernel, total),
        (shape(plain, bf16), shape(plain, bf16), shape(plain, bf16), shape((2, width), f32)),
        n_in=10,
        cost=aside,
    )(near, far, mixed_t, res_t, q_t, sg_t, gain_row, cotangent, key_feats, value_feats)
    side_z, side_y, side_x = sides
    ends = sum_over(ends, "seq", side_x, 1)
    lag_sent = run_lag(grad_received, skip_here, spectra, ends)
    late = pl.CostEstimate(flops=3 * 10**10, bytes_accessed=10**8, transcendentals=0)
    ends = sum_over(ends, "seq", 2, side_x, late)
    ends = sum_over(ends, "seq", side_y // 2, 2 * side_x)
    ends = sum_over(ends, "seq", side_z, side_x * side_y)
    lag_received = exchange(lag_sent)
    grad_key, grad_value, grad_filter = call(
        finish_kernel,
        (shape(plain, bf16), shape(plain, bf16), shape(plain, f32)),
        n_in=3,
        hbm_out=(0, 1, 2),
        scratch=(vm(plain, bf16), vm(plain, bf16), vm(plain, f32), dma((parts, 3))),
    )(lag_received, key_feats, value_feats)
    return (
        normed,
        grad_residual,
        grad_query,
        grad_key,
        grad_value,
        grad_filter,
        ends[0],
        ends[1],
    )


def solution(mesh):
    return jax.shard_map(
        on_device,
        mesh=mesh,
        in_specs=(P("seq", "chan"),) * 6 + (P("chan"),) * 2,
        out_specs=(P("seq", "chan"),) * 6 + (P("chan"),) * 2,
        check_vma=False,
    )
```

```python
import functools
import math

import jax
import jax.numpy as jnp
import ml_dtypes
import numpy as np
from jax import lax
from jax.experimental import pallas as pl
from jax.experimental.pallas import tpu as pltpu
from jax.sharding import PartitionSpec as P

epsilon = 1e-06
f32 = jnp.float32
bf16 = jnp.bfloat16


def split_host(table):
    high = table.astype(ml_dtypes.bfloat16)
    low = (table - high.astype(np.float64)).astype(ml_dtypes.bfloat16)
    return high, low


@functools.cache
def tables(blocks, lanes):
    length = 2 * blocks * lanes
    k1 = np.arange(blocks)[:, None] + 0.5
    a = np.arange(blocks)[None, :]
    angle = 2.0 * np.pi * k1 * a / (2 * blocks)
    outer = np.concatenate((np.cos(angle), -np.sin(angle)), 0)
    outer_high, outer_low = split_host(outer)
    first = np.concatenate((outer_high, outer_low), 1)
    back = outer.T * (2.0 / length)
    back_high, back_low = split_host(back)
    last = np.concatenate((back_high, back_low, back_high), 1)
    b = np.arange(lanes)[None, :]
    angle = 2.0 * np.pi * k1 * b / length
    twiddle = np.concatenate((np.cos(angle), np.sin(angle)), 0).astype(np.float32)
    angle = 2.0 * np.pi * (np.arange(lanes)[:, None] * b % lanes) / lanes
    cosine, sine = np.cos(angle), np.sin(angle)
    inner = np.block([[cosine, -sine], [sine, cosine]])
    inner_high, inner_low = split_host(inner)
    inner = np.concatenate((inner_high, inner_high, inner_low), 0)
    inverse_high, inverse_low = inner_high.T, inner_low.T
    inverse = np.concatenate((inverse_high, inverse_high, inverse_low), 0)
    return (first, last, twiddle, inner, inverse)


def split(values):
    high = values.astype(bf16)
    low = (values - high.astype(f32)).astype(bf16)
    return high, low


def matmul(left, right):
    return jnp.dot(left, right, preferred_element_type=f32)


def put(u_ref, here, offset, values):
    high, low = split(values)
    width = u_ref.shape[1] // 2
    lanes = values.shape[1]
    u_ref[here, offset : offset + lanes] = high
    u_ref[here, width + offset : width + offset + lanes] = low


def forward(series_ref, stride, rows, first_ref, twiddle_ref, inner_ref, u_ref, out_ref, copies=()):
    blocks = first_ref.shape[0] // 2
    lanes = twiddle_ref.shape[1]
    cosine = twiddle_ref[:blocks]
    sine = twiddle_ref[blocks:]
    for pair in range(rows // 2):
        columns = []
        for row in (2 * pair, 2 * pair + 1):
            x = series_ref[pl.ds(row, blocks, stride=stride), :].astype(bf16)
            columns.append(jnp.concatenate((x, x), 0))
        out = matmul(first_ref[...], jnp.concatenate(columns, 1))
        for i in range(2):
            re = out[:blocks, i * lanes : (i + 1) * lanes]
            im = out[blocks:, i * lanes : (i + 1) * lanes]
            here = pl.ds((2 * pair + i) * blocks, blocks)
            put(u_ref, here, 0, re * cosine + im * sine)
            put(u_ref, here, lanes, im * cosine - re * sine)
    n = 2 * lanes
    chunk = 4 * blocks
    for i in range(rows // 4):
        c = pl.ds(i * chunk, chunk)
        out_ref[c] = matmul(u_ref[c, : 2 * n], inner_ref[: 2 * n]) + matmul(
            u_ref[c, :n], inner_ref[2 * n :]
        )
        if copies:
            copies[i].start()


def inverse(rows, last_ref, twiddle_ref, inverse_ref, u_ref, z_ref, out_ref, stride, base=0):
    blocks = last_ref.shape[0]
    lanes = twiddle_ref.shape[1]
    cosine = twiddle_ref[:blocks]
    sine = twiddle_ref[blocks:]
    n = 2 * lanes
    chunk = 4 * blocks
    for i in range(rows // 4):
        c = pl.ds(base * blocks + i * chunk, chunk)
        z_ref[c] = matmul(u_ref[c, : 2 * n], inverse_ref[: 2 * n]) + matmul(
            u_ref[c, :n], inverse_ref[2 * n :]
        )
    for pair in range(rows // 2):
        columns = []
        for row in (2 * pair, 2 * pair + 1):
            re = z_ref[pl.ds((base + row) * blocks, blocks), :lanes]
            im = z_ref[pl.ds((base + row) * blocks, blocks), lanes:]
            zh, zl = split(
                jnp.concatenate((re * cosine - im * sine, im * cosine + re * sine), 0)
            )
            columns.append(jnp.concatenate((zh, zh, zl), 0))
        out = matmul(last_ref[...], jnp.concatenate(columns, 1))
        for i in range(2):
            out_ref[pl.ds(base + 2 * pair + i, blocks, stride=stride), :] = out[
                :, i * lanes : (i + 1) * lanes
            ]


def copies_of(source_ref, target_ref, sems):
    count = sems.shape[0]
    chunk = source_ref.shape[0] // count
    return [
        pltpu.make_async_copy(
            source_ref.at[pl.ds(i * chunk, chunk)],
            target_ref.at[pl.ds(i * chunk, chunk)],
            sems.at[i],
        )
        for i in range(count)
    ]


def conv_kernel(
    recv_ref, skip_ref, first_ref, last_ref, twiddle_ref, inner_ref, inverse_ref,
    mixed_ref, kept_ref, spec_ref, x_ref, u_ref, z_ref, y_ref, sems,
):
    blocks, rows, lanes = recv_ref.shape
    channels = rows // 2
    half = channels * blocks
    wide = rows + 8
    for a in range(blocks):
        x_ref[pl.ds(a * wide, rows), :] = recv_ref[a].astype(f32)
    copies = copies_of(spec_ref, kept_ref, sems)
    forward(x_ref, wide, rows, first_ref, twiddle_ref, inner_ref, u_ref, spec_ref, copies)
    for c in range(channels):
        prod = pl.ds(c * blocks, blocks)
        filt = pl.ds(half + c * blocks, blocks)
        fre = spec_ref[filt, :lanes] + skip_ref[c]
        fim = spec_ref[filt, lanes:]
        pre, pim = spec_ref[prod, :lanes], spec_ref[prod, lanes:]
        put(u_ref, prod, 0, pre * fre - pim * fim)
        put(u_ref, prod, lanes, pre * fim + pim * fre)
    wide = channels + 8
    inverse(channels, last_ref, twiddle_ref, inverse_ref, u_ref, z_ref, y_ref, wide)
    for a in range(blocks):
        mixed_ref[a] = y_ref[pl.ds(a * wide, channels), :].astype(bf16)
    for copy in copies:
        copy.wait()


def lag_kernel(
    recv_ref, skip_ref, first_ref, last_ref, twiddle_ref, inner_ref, inverse_ref, kept_ref, *rest
):
    out_ref, spec_ref, x_ref, g_ref, u_ref, z_ref, y_ref, ready_ref, sems, out_sems = rest[-10:]
    blocks, channels, lanes = recv_ref.shape
    rows = 2 * channels
    half = channels * blocks
    copies = copies_of(kept_ref, spec_ref, sems)
    ahead = len(copies) // 2
    for i in range(ahead):
        copies[ahead + i].start()
    for i in range(ahead):
        copies[i].start()
    wide = channels + 8
    for a in range(blocks):
        x_ref[pl.ds(a * wide, channels), :] = recv_ref[a].astype(f32)
    forward(x_ref, wide, channels, first_ref, twiddle_ref, inner_ref, u_ref, g_ref)
    wide = rows + 8
    leaving = []
    for source, target, lead in ((half, 0, ahead), (0, half, 0)):
        for c in range(channels):
            if c % (channels // ahead) == 0:
                copies[lead + c * ahead // channels].wait()
            grad = pl.ds(c * blocks, blocks)
            gre, gim = g_ref[grad, :lanes], g_ref[grad, lanes:]
            here = pl.ds(source + c * blocks, blocks)
            sre, sim = spec_ref[here, :lanes], spec_ref[here, lanes:]
            if source:
                sre = sre + skip_ref[c]
            put(u_ref, pl.ds(target + c * blocks, blocks), 0, sre * gre + sim * gim)
            put(u_ref, pl.ds(target + c * blocks, blocks), lanes, sre * gim - sim * gre)
        inverse(
            channels, last_ref, twiddle_ref, inverse_ref, u_ref, z_ref, y_ref, wide, target // blocks
        )
        first = target // blocks
        for a in range(blocks):
            ready_ref[first // channels, a] = y_ref[pl.ds(a * wide + first, channels), :].astype(bf16)
        leaving.append(
            pltpu.make_async_copy(
                ready_ref.at[first // channels],
                out_ref.at[:, pl.ds(first, channels), :],
                out_sems.at[first // channels],
            )
        )
        leaving[-1].start()
    for copy in leaving:
        copy.wait()


def send_kernel(
    key_hbm, value_hbm, filters_hbm, out_hbm, key_ref, value_ref, filters_ref, out_ref, sems, out_sems
):
    tokens, width = key_ref.shape
    peers, rows, _ = out_ref.shape
    channels = rows // 2
    group = tokens // channels
    parts = out_sems.shape[0]
    arriving = []
    for part in range(parts):
        cols = pl.ds(part * (width // parts), width // parts)
        pairs = ((key_hbm, key_ref), (value_hbm, value_ref), (filters_hbm, filters_ref))
        arriving.append(
            [
                pltpu.make_async_copy(source.at[:, cols], target.at[:, cols], sems.at[part, i])
                for i, (source, target) in enumerate(pairs)
            ]
        )
        for copy in arriving[-1]:
            copy.start()
    leaving = []
    for part in range(parts):
        for copy in arriving[part]:
            copy.wait()
        steps = width // tokens // parts
        for j in range(part * steps, (part + 1) * steps):
            cols = pl.ds(j * tokens, tokens)
            dest = pl.ds(j * group, group)
            product = key_ref[:, cols].astype(f32) * value_ref[:, cols].astype(f32)
            out_ref[dest, :channels, :] = product.astype(bf16).T.reshape(group, channels, tokens)
            out_ref[dest, channels:, :] = filters_ref[:, cols].T.reshape(group, channels, tokens)
        dest = pl.ds(part * (peers // parts), peers // parts)
        leaving.append(
            pltpu.make_async_copy(out_ref.at[dest], out_hbm.at[dest], out_sems.at[part])
        )
        leaving[-1].start()
    for copy in leaving:
        copy.wait()


def turn_kernel(residual_ref, query_ref, cotangent_ref, gain_ref, res_ref, q_ref, sg_ref):
    tokens, width = residual_ref.shape
    for j in range(width // tokens):
        cols = pl.ds(j * tokens, tokens)
        res_ref[cols, :] = residual_ref[:, cols].T
        q_ref[cols, :] = query_ref[:, cols].T
        sg_ref[cols, :] = (cotangent_ref[:, cols].astype(f32) * gain_ref[:, cols]).T


def sums_kernel(mixed_ref, res_ref, q_ref, sg_ref, out_ref):
    width, tokens = res_ref.shape
    summed = res_ref[...].astype(f32) + q_ref[...].astype(f32) * mixed_ref[...].astype(f32)
    out_ref[0:1, :] = jnp.sum(summed * summed, axis=0, keepdims=True)
    out_ref[1:2, :] = jnp.sum(sg_ref[...] * summed, axis=0, keepdims=True)


def norm_terms(sums_refs, total):
    near, far = sums_refs
    sums = (near[...] + far[...]) * (1.0 / total)
    inv_rms = lax.rsqrt(sums[0:1, :] + epsilon)
    alpha = inv_rms * inv_rms * inv_rms * sums[1:2, :]
    return inv_rms, alpha


def grad_kernel(total, near_ref, far_ref, mixed_ref, res_ref, q_ref, sg_ref, out_hbm, out_ref, sems):
    inv_rms, alpha = norm_terms((near_ref, far_ref), total)
    parts = sems.shape[0]
    size = res_ref.shape[0] // parts
    leaving = []
    for part in range(parts):
        here = pl.ds(part * size, size)
        query = q_ref[here].astype(f32)
        summed = res_ref[here].astype(f32) + query * mixed_ref[here].astype(f32)
        grad_summed = inv_rms * sg_ref[here] - summed * alpha
        out_ref[here] = (grad_summed * query).astype(bf16)
        leaving.append(
            pltpu.make_async_copy(out_ref.at[here], out_hbm.at[here], sems.at[part])
        )
        leaving[-1].start()
    for copy in leaving:
        copy.wait()


def ends_kernel(
    total, near_ref, far_ref, mixed_ref, res_ref, q_ref, sg_ref, cotangent_ref, key_ref, value_ref,
    ends_ref,
):
    width, tokens = res_ref.shape
    inv_rms, alpha = norm_terms((near_ref, far_ref), total)
    for j in range(width // tokens):
        cols = pl.ds(j * tokens, tokens)
        query = q_ref[cols, :].astype(f32)
        summed = res_ref[cols, :].astype(f32) + query * mixed_ref[cols, :].astype(f32)
        grad_summed = inv_rms * sg_ref[cols, :] - summed * alpha
        unit = (summed * inv_rms).T
        grad_mixed = (grad_summed * query).astype(bf16).T.astype(f32)
        product = key_ref[:, cols].astype(f32) * value_ref[:, cols].astype(f32)
        product = product.astype(bf16).astype(f32)
        ends_ref[0:1, cols] = jnp.sum(grad_mixed * product, axis=0, keepdims=True)
        ends_ref[1:2, cols] = jnp.sum(
            cotangent_ref[:, cols].astype(f32) * unit, axis=0, keepdims=True
        )


def norm_kernel(
    total, near_ref, far_ref, mixed_ref, res_ref, q_ref, sg_ref, gain_ref,
    normed_ref, gres_ref, gq_ref,
):
    width, tokens = res_ref.shape
    inv_rms, alpha = norm_terms((near_ref, far_ref), total)
    for j in range(width // tokens):
        cols = pl.ds(j * tokens, tokens)
        mixed = mixed_ref[cols, :].astype(f32)
        summed = res_ref[cols, :].astype(f32) + q_ref[cols, :].astype(f32) * mixed
        grad_summed = inv_rms * sg_ref[cols, :] - summed * alpha
        normed_ref[:, cols] = ((summed * inv_rms).T * gain_ref[:, cols]).astype(bf16)
        gres_ref[:, cols] = grad_summed.astype(bf16).T
        gq_ref[:, cols] = (grad_summed * mixed).astype(bf16).T


def finish_kernel(
    recv_ref, key_ref, value_ref, gk_hbm, gv_hbm, gf_hbm, gk_ref, gv_ref, gf_ref, sems
):
    tokens, width = key_ref.shape
    peers, rows, _ = recv_ref.shape
    channels = rows // 2
    group = tokens // channels
    parts = sems.shape[0]
    steps = width // tokens // parts
    leaving = []
    for part in range(parts):
        for j in range(part * steps, (part + 1) * steps):
            cols = pl.ds(j * tokens, tokens)
            dest = pl.ds(j * group, group)
            back = recv_ref[dest, :channels, :].reshape(tokens, tokens).T.astype(f32)
            gk_ref[:, cols] = (back * value_ref[:, cols].astype(f32)).astype(bf16)
            gv_ref[:, cols] = (back * key_ref[:, cols].astype(f32)).astype(bf16)
            gf_ref[:, cols] = recv_ref[dest, channels:, :].reshape(tokens, tokens).T.astype(f32)
        cols = pl.ds(part * (width // parts), width // parts)
        pairs = ((gk_ref, gk_hbm), (gv_ref, gv_hbm), (gf_ref, gf_hbm))
        for i, (source, target) in enumerate(pairs):
            leaving.append(
                pltpu.make_async_copy(source.at[:, cols], target.at[:, cols], sems.at[part, i])
            )
            leaving[-1].start()
    for copy in leaving:
        copy.wait()


def places(side, stride, count, step):
    pairs = []
    for source in range(count):
        place = source // stride % side
        pairs.append((source, source + ((place + step) % side - place) * stride))
    return pairs


def add_kernel(*refs):
    *sources, out_ref = refs
    own, *others = (ref[...] for ref in sources)
    out_ref[...] = sum(others, own)


def sum_over(values, axis, side, stride, cost=None):
    count = lax.axis_size(axis)
    moved = [
        lax.ppermute(values, axis, places(side, stride, count, step)) for step in range(1, side)
    ]
    if cost is not None:
        out = shape(values.shape, values.dtype)
        return call(add_kernel, out, n_in=side, cost=cost)(values, *moved)
    for part in moved:
        values = values + part
    return values


def call(kernel, out_shape, n_in, scratch=(), cost=None, smem=(), hbm=(), hbm_out=()):
    def place(i, scalar, far):
        space = pltpu.SMEM if i in scalar else pltpu.HBM if i in far else pltpu.VMEM
        return pl.BlockSpec(memory_space=space)

    outs = out_shape if isinstance(out_shape, tuple) else (out_shape,)
    out_specs = tuple(place(i, (), hbm_out) for i in range(len(outs)))
    return pl.pallas_call(
        kernel,
        out_shape=out_shape,
        in_specs=[place(i, smem, hbm) for i in range(n_in)],
        out_specs=out_specs if isinstance(out_shape, tuple) else out_specs[0],
        scratch_shapes=list(scratch),
        compiler_params=pltpu.CompilerParams(vmem_limit_bytes=48 * 1024 * 1024),
        cost_estimate=cost,
    )


def far_memory(values):
    return pltpu.with_memory_space_constraint(values, pltpu.HBM)


def shape(dims, dtype):
    return jax.ShapeDtypeStruct(dims, dtype)


def run_conv(received, skip_here):
    peers, rows, tokens = received.shape
    channels = rows // 2
    half = channels * peers
    spectra_shape = (2 * half, 2 * tokens)
    vm = pltpu.VMEM
    return call(
        conv_kernel,
        (shape((peers, channels, tokens), bf16), pltpu.HBM(spectra_shape, f32)),
        n_in=7,
        smem=(1,),
        hbm_out=(1,),
        scratch=(
            vm(spectra_shape, f32),
            vm((2 * half + 8 * peers, tokens), f32),
            vm((2 * half, 4 * tokens), bf16),
            vm((half, 2 * tokens), f32),
            vm((half + 8 * peers, tokens), f32),
            pltpu.SemaphoreType.DMA((rows // 4,)),
        ),
    )(received, skip_here, *tables(peers, tokens))


def run_lag(received, skip_here, spectra, *after):
    peers, channels, tokens = received.shape
    half = channels * peers
    spectra_shape = (2 * half, 2 * tokens)
    vm = pltpu.VMEM
    return call(
        lag_kernel,
        pltpu.HBM((peers, 2 * channels, tokens), bf16),
        n_in=8 + len(after),
        smem=(1,),
        hbm=(7, 8),
        hbm_out=(0,),
        scratch=(
            vm(spectra_shape, f32),
            vm((half + 8 * peers, tokens), f32),
            vm((half, 2 * tokens), f32),
            vm((2 * half, 4 * tokens), bf16),
            vm(spectra_shape, f32),
            vm((2 * half + 8 * peers, tokens), f32),
            vm((2, peers, channels, tokens), bf16),
            pltpu.SemaphoreType.DMA((channels // 2,)),
            pltpu.SemaphoreType.DMA((2,)),
        ),
    )(received, skip_here, *tables(peers, tokens), far_memory(spectra), *after)


sides = (4, 4, 4)


def on_device(
    residual, query_feats, key_feats, value_feats, filters, cotangent, skip_bias, norm_gain
):
    tokens, width = residual.shape
    peers = lax.axis_size("seq")
    total = float(width * lax.axis_size("chan"))
    channels = width // peers
    vm = pltpu.VMEM

    def exchange(values):
        return lax.all_to_all(values, "seq", split_axis=0, concat_axis=0, tiled=True)

    plain = (tokens, width)
    turned = (width, tokens)
    dma = pltpu.SemaphoreType.DMA
    aside = pl.CostEstimate(flops=10**6, bytes_accessed=4 * 10**6, transcendentals=0)
    parts = 4
    sent = call(
        send_kernel,
        pltpu.HBM((peers, 2 * channels, tokens), bf16),
        n_in=3,
        hbm=(0, 1, 2),
        hbm_out=(0,),
        scratch=(
            vm(plain, bf16),
            vm(plain, bf16),
            vm(plain, bf16),
            vm((peers, 2 * channels, tokens), bf16),
            dma((parts, 3)),
            dma((parts,)),
        ),
    )(far_memory(key_feats), far_memory(value_feats), far_memory(filters))
    received = exchange(sent)
    gain_row = norm_gain[None, :]
    res_t, q_t, sg_t = call(
        turn_kernel,
        (shape(turned, bf16), shape(turned, bf16), shape(turned, f32)),
        n_in=4,
        cost=aside,
    )(residual, query_feats, cotangent, gain_row)
    skip_here = lax.dynamic_slice_in_dim(skip_bias, lax.axis_index("seq") * channels, channels)
    mixed_sent, spectra = run_conv(received, skip_here)
    mixed_t = exchange(mixed_sent).reshape(width, tokens)
    sums = call(sums_kernel, shape((2, tokens), f32), n_in=4)(mixed_t, res_t, q_t, sg_t)
    near = sum_over(sums, "chan", 2, 1)
    far = lax.ppermute(near, "chan", places(2, 2, 4, 1))
    grad_sent = call(
        functools.partial(grad_kernel, total),
        pltpu.HBM(turned, bf16),
        n_in=6,
        hbm_out=(0,),
        scratch=(vm(turned, bf16), dma((parts,))),
    )(near, far, mixed_t, res_t, q_t, sg_t)
    grad_received = exchange(grad_sent.reshape(peers, channels, tokens))
    ends = call(
        functools.partial(ends_kernel, total), shape((2, width), f32), n_in=9, cost=aside
    )(near, far, mixed_t, res_t, q_t, sg_t, cotangent, key_feats, value_feats)
    normed, grad_residual, grad_query = call(
        functools.partial(norm_kernel, total),
        (shape(plain, bf16), shape(plain, bf16), shape(plain, bf16)),
        n_in=7,
        cost=aside,
    )(near, far, mixed_t, res_t, q_t, sg_t, gain_row)
    side_z, side_y, side_x = sides
    ends = sum_over(ends, "seq", side_x, 1)
    lag_sent = run_lag(grad_received, skip_here, spectra, ends)
    late = pl.CostEstimate(flops=3 * 10**10, bytes_accessed=10**8, transcendentals=0)
    ends = sum_over(ends, "seq", 2, side_x, late)
    ends = sum_over(ends, "seq", side_y // 2, 2 * side_x)
    ends = sum_over(ends, "seq", side_z, side_x * side_y)
    lag_received = exchange(lag_sent)
    grad_key, grad_value, grad_filter = call(
        finish_kernel,
        (shape(plain, bf16), shape(plain, bf16), shape(plain, f32)),
        n_in=3,
        hbm_out=(0, 1, 2),
        scratch=(vm(plain, bf16), vm(plain, bf16), vm(plain, f32), dma((parts, 3))),
    )(lag_received, key_feats, value_feats)
    return (
        normed,
        grad_residual,
        grad_query,
        grad_key,
        grad_value,
        grad_filter,
        ends[0],
        ends[1],
    )


def solution(mesh):
    return jax.shard_map(
        on_device,
        mesh=mesh,
        in_specs=(P("seq", "chan"),) * 6 + (P("chan"),) * 2,
        out_specs=(P("seq", "chan"),) * 6 + (P("chan"),) * 2,
        check_vma=False,
    )
```

```python
import functools
import math

import jax
import jax.numpy as jnp
import ml_dtypes
import numpy as np
from jax import lax
from jax.experimental import pallas as pl
from jax.experimental.pallas import tpu as pltpu
from jax.sharding import PartitionSpec as P

epsilon = 1e-06
f32 = jnp.float32
bf16 = jnp.bfloat16


def split_host(table):
    high = table.astype(ml_dtypes.bfloat16)
    low = (table - high.astype(np.float64)).astype(ml_dtypes.bfloat16)
    return high, low


@functools.cache
def tables(blocks, lanes):
    length = 2 * blocks * lanes
    k1 = np.arange(blocks)[:, None] + 0.5
    a = np.arange(blocks)[None, :]
    angle = 2.0 * np.pi * k1 * a / (2 * blocks)
    outer = np.concatenate((np.cos(angle), -np.sin(angle)), 0)
    outer_high, outer_low = split_host(outer)
    first = np.concatenate((outer_high, outer_low), 1)
    back = outer.T * (2.0 / length)
    back_high, back_low = split_host(back)
    last = np.concatenate((back_high, back_low, back_high), 1)
    b = np.arange(lanes)[None, :]
    angle = 2.0 * np.pi * k1 * b / length
    twiddle = np.concatenate((np.cos(angle), np.sin(angle)), 0).astype(np.float32)
    angle = 2.0 * np.pi * (np.arange(lanes)[:, None] * b % lanes) / lanes
    cosine, sine = np.cos(angle), np.sin(angle)
    inner = np.block([[cosine, -sine], [sine, cosine]])
    inner_high, inner_low = split_host(inner)
    inner = np.concatenate((inner_high, inner_high, inner_low), 0)
    inverse_high, inverse_low = inner_high.T, inner_low.T
    inverse = np.concatenate((inverse_high, inverse_high, inverse_low), 0)
    return (first, last, twiddle, inner, inverse)


def split(values):
    high = values.astype(bf16)
    low = (values - high.astype(f32)).astype(bf16)
    return high, low


def matmul(left, right):
    return jnp.dot(left, right, preferred_element_type=f32)


def put(u_ref, here, offset, values):
    high, low = split(values)
    width = u_ref.shape[1] // 2
    lanes = values.shape[1]
    u_ref[here, offset : offset + lanes] = high
    u_ref[here, width + offset : width + offset + lanes] = low


def forward(series_ref, stride, rows, first_ref, twiddle_ref, inner_ref, u_ref, out_ref, copies=()):
    blocks = first_ref.shape[0] // 2
    lanes = twiddle_ref.shape[1]
    cosine = twiddle_ref[:blocks]
    sine = twiddle_ref[blocks:]
    for pair in range(rows // 2):
        columns = []
        for row in (2 * pair, 2 * pair + 1):
            x = series_ref[pl.ds(row, blocks, stride=stride), :].astype(bf16)
            columns.append(jnp.concatenate((x, x), 0))
        out = matmul(first_ref[...], jnp.concatenate(columns, 1))
        for i in range(2):
            re = out[:blocks, i * lanes : (i + 1) * lanes]
            im = out[blocks:, i * lanes : (i + 1) * lanes]
            here = pl.ds((2 * pair + i) * blocks, blocks)
            put(u_ref, here, 0, re * cosine + im * sine)
            put(u_ref, here, lanes, im * cosine - re * sine)
    n = 2 * lanes
    chunk = 4 * blocks
    for i in range(rows // 4):
        c = pl.ds(i * chunk, chunk)
        out_ref[c] = matmul(u_ref[c, : 2 * n], inner_ref[: 2 * n]) + matmul(
            u_ref[c, :n], inner_ref[2 * n :]
        )
        if copies:
            copies[i].start()


def inverse(rows, last_ref, twiddle_ref, inverse_ref, u_ref, z_ref, out_ref, stride, base=0):
    blocks = last_ref.shape[0]
    lanes = twiddle_ref.shape[1]
    cosine = twiddle_ref[:blocks]
    sine = twiddle_ref[blocks:]
    n = 2 * lanes
    chunk = 4 * blocks
    for i in range(rows // 4):
        c = pl.ds(base * blocks + i * chunk, chunk)
        z_ref[c] = matmul(u_ref[c, : 2 * n], inverse_ref[: 2 * n]) + matmul(
            u_ref[c, :n], inverse_ref[2 * n :]
        )
    for pair in range(rows // 2):
        columns = []
        for row in (2 * pair, 2 * pair + 1):
            re = z_ref[pl.ds((base + row) * blocks, blocks), :lanes]
            im = z_ref[pl.ds((base + row) * blocks, blocks), lanes:]
            zh, zl = split(
                jnp.concatenate((re * cosine - im * sine, im * cosine + re * sine), 0)
            )
            columns.append(jnp.concatenate((zh, zh, zl), 0))
        out = matmul(last_ref[...], jnp.concatenate(columns, 1))
        for i in range(2):
            out_ref[pl.ds(base + 2 * pair + i, blocks, stride=stride), :] = out[
                :, i * lanes : (i + 1) * lanes
            ]


def copies_of(source_ref, target_ref, sems):
    count = sems.shape[0]
    chunk = source_ref.shape[0] // count
    return [
        pltpu.make_async_copy(
            source_ref.at[pl.ds(i * chunk, chunk)],
            target_ref.at[pl.ds(i * chunk, chunk)],
            sems.at[i],
        )
        for i in range(count)
    ]


def conv_kernel(
    recv_ref, skip_ref, first_ref, last_ref, twiddle_ref, inner_ref, inverse_ref,
    mixed_ref, kept_ref, spec_ref, x_ref, u_ref, z_ref, y_ref, ready_ref, sems, out_sems,
):
    blocks, rows, lanes = recv_ref.shape
    channels = rows // 2
    half = channels * blocks
    wide = rows + 8
    for a in range(blocks):
        x_ref[pl.ds(a * wide, rows), :] = recv_ref[a].astype(f32)
    copies = copies_of(spec_ref, kept_ref, sems)
    forward(x_ref, wide, rows, first_ref, twiddle_ref, inner_ref, u_ref, spec_ref, copies)
    for c in range(channels):
        prod = pl.ds(c * blocks, blocks)
        filt = pl.ds(half + c * blocks, blocks)
        fre = spec_ref[filt, :lanes] + skip_ref[c]
        fim = spec_ref[filt, lanes:]
        pre, pim = spec_ref[prod, :lanes], spec_ref[prod, lanes:]
        put(u_ref, prod, 0, pre * fre - pim * fim)
        put(u_ref, prod, lanes, pre * fim + pim * fre)
    wide = channels + 8
    inverse(channels, last_ref, twiddle_ref, inverse_ref, u_ref, z_ref, y_ref, wide)
    leaving = copies_of(ready_ref, mixed_ref, out_sems)
    size = blocks // len(leaving)
    for a in range(blocks):
        ready_ref[a] = y_ref[pl.ds(a * wide, channels), :].astype(bf16)
        if a % size == size - 1:
            leaving[a // size].start()
    for copy in copies + leaving:
        copy.wait()


def lag_kernel(
    recv_ref, skip_ref, first_ref, last_ref, twiddle_ref, inner_ref, inverse_ref, kept_ref, *rest
):
    out_ref, spec_ref, x_ref, g_ref, u_ref, z_ref, y_ref, ready_ref, sems, out_sems = rest[-10:]
    blocks, channels, lanes = recv_ref.shape
    rows = 2 * channels
    half = channels * blocks
    copies = copies_of(kept_ref, spec_ref, sems)
    ahead = len(copies) // 2
    for i in range(ahead):
        copies[ahead + i].start()
    for i in range(ahead):
        copies[i].start()
    wide = channels + 8
    for a in range(blocks):
        x_ref[pl.ds(a * wide, channels), :] = recv_ref[a].astype(f32)
    forward(x_ref, wide, channels, first_ref, twiddle_ref, inner_ref, u_ref, g_ref)
    wide = rows + 8
    leaving = []
    for source, target, lead in ((half, 0, ahead), (0, half, 0)):
        for c in range(channels):
            if c % (channels // ahead) == 0:
                copies[lead + c * ahead // channels].wait()
            grad = pl.ds(c * blocks, blocks)
            gre, gim = g_ref[grad, :lanes], g_ref[grad, lanes:]
            here = pl.ds(source + c * blocks, blocks)
            sre, sim = spec_ref[here, :lanes], spec_ref[here, lanes:]
            if source:
                sre = sre + skip_ref[c]
            put(u_ref, pl.ds(target + c * blocks, blocks), 0, sre * gre + sim * gim)
            put(u_ref, pl.ds(target + c * blocks, blocks), lanes, sre * gim - sim * gre)
        inverse(
            channels, last_ref, twiddle_ref, inverse_ref, u_ref, z_ref, y_ref, wide, target // blocks
        )
        first = target // blocks
        for a in range(blocks):
            ready_ref[first // channels, a] = y_ref[pl.ds(a * wide + first, channels), :].astype(bf16)
        leaving.append(
            pltpu.make_async_copy(
                ready_ref.at[first // channels],
                out_ref.at[:, pl.ds(first, channels), :],
                out_sems.at[first // channels],
            )
        )
        leaving[-1].start()
    for copy in leaving:
        copy.wait()


def send_kernel(
    key_hbm, value_hbm, filters_hbm, out_hbm, key_ref, value_ref, filters_ref, out_ref, sems, out_sems
):
    tokens, width = key_ref.shape
    peers, rows, _ = out_ref.shape
    channels = rows // 2
    group = tokens // channels
    parts = out_sems.shape[0]
    arriving = []
    for part in range(parts):
        cols = pl.ds(part * (width // parts), width // parts)
        pairs = ((key_hbm, key_ref), (value_hbm, value_ref), (filters_hbm, filters_ref))
        arriving.append(
            [
                pltpu.make_async_copy(source.at[:, cols], target.at[:, cols], sems.at[part, i])
                for i, (source, target) in enumerate(pairs)
            ]
        )
        for copy in arriving[-1]:
            copy.start()
    leaving = []
    for part in range(parts):
        for copy in arriving[part]:
            copy.wait()
        steps = width // tokens // parts
        for j in range(part * steps, (part + 1) * steps):
            cols = pl.ds(j * tokens, tokens)
            dest = pl.ds(j * group, group)
            product = key_ref[:, cols].astype(f32) * value_ref[:, cols].astype(f32)
            out_ref[dest, :channels, :] = product.astype(bf16).T.reshape(group, channels, tokens)
            out_ref[dest, channels:, :] = filters_ref[:, cols].T.reshape(group, channels, tokens)
        dest = pl.ds(part * (peers // parts), peers // parts)
        leaving.append(
            pltpu.make_async_copy(out_ref.at[dest], out_hbm.at[dest], out_sems.at[part])
        )
        leaving[-1].start()
    for copy in leaving:
        copy.wait()


def turn_kernel(residual_ref, query_ref, cotangent_ref, gain_ref, res_ref, q_ref, sg_ref):
    tokens, width = residual_ref.shape
    for j in range(width // tokens):
        cols = pl.ds(j * tokens, tokens)
        res_ref[cols, :] = residual_ref[:, cols].T
        q_ref[cols, :] = query_ref[:, cols].T
        sg_ref[cols, :] = (cotangent_ref[:, cols].astype(f32) * gain_ref[:, cols]).T


def sums_kernel(mixed_ref, res_ref, q_ref, sg_ref, out_ref):
    width, tokens = res_ref.shape
    summed = res_ref[...].astype(f32) + q_ref[...].astype(f32) * mixed_ref[...].astype(f32)
    out_ref[0:1, :] = jnp.sum(summed * summed, axis=0, keepdims=True)
    out_ref[1:2, :] = jnp.sum(sg_ref[...] * summed, axis=0, keepdims=True)


def norm_terms(sums_refs, total):
    near, far = sums_refs
    sums = (near[...] + far[...]) * (1.0 / total)
    inv_rms = lax.rsqrt(sums[0:1, :] + epsilon)
    alpha = inv_rms * inv_rms * inv_rms * sums[1:2, :]
    return inv_rms, alpha


def grad_kernel(total, near_ref, far_ref, mixed_ref, res_ref, q_ref, sg_ref, out_hbm, out_ref, sems):
    inv_rms, alpha = norm_terms((near_ref, far_ref), total)
    parts = sems.shape[0]
    size = res_ref.shape[0] // parts
    leaving = []
    for part in range(parts):
        here = pl.ds(part * size, size)
        query = q_ref[here].astype(f32)
        summed = res_ref[here].astype(f32) + query * mixed_ref[here].astype(f32)
        grad_summed = inv_rms * sg_ref[here] - summed * alpha
        out_ref[here] = (grad_summed * query).astype(bf16)
        leaving.append(
            pltpu.make_async_copy(out_ref.at[here], out_hbm.at[here], sems.at[part])
        )
        leaving[-1].start()
    for copy in leaving:
        copy.wait()


def ends_kernel(
    total, near_ref, far_ref, mixed_ref, res_ref, q_ref, sg_ref, cotangent_ref, key_ref, value_ref,
    ends_ref,
):
    width, tokens = res_ref.shape
    inv_rms, alpha = norm_terms((near_ref, far_ref), total)
    for j in range(width // tokens):
        cols = pl.ds(j * tokens, tokens)
        query = q_ref[cols, :].astype(f32)
        summed = res_ref[cols, :].astype(f32) + query * mixed_ref[cols, :].astype(f32)
        grad_summed = inv_rms * sg_ref[cols, :] - summed * alpha
        unit = (summed * inv_rms).T
        grad_mixed = (grad_summed * query).astype(bf16).T.astype(f32)
        product = key_ref[:, cols].astype(f32) * value_ref[:, cols].astype(f32)
        product = product.astype(bf16).astype(f32)
        ends_ref[0:1, cols] = jnp.sum(grad_mixed * product, axis=0, keepdims=True)
        ends_ref[1:2, cols] = jnp.sum(
            cotangent_ref[:, cols].astype(f32) * unit, axis=0, keepdims=True
        )


def norm_kernel(
    total, near_ref, far_ref, mixed_ref, res_ref, q_ref, sg_ref, gain_ref,
    normed_ref, gres_ref, gq_ref,
):
    width, tokens = res_ref.shape
    inv_rms, alpha = norm_terms((near_ref, far_ref), total)
    for j in range(width // tokens):
        cols = pl.ds(j * tokens, tokens)
        mixed = mixed_ref[cols, :].astype(f32)
        summed = res_ref[cols, :].astype(f32) + q_ref[cols, :].astype(f32) * mixed
        grad_summed = inv_rms * sg_ref[cols, :] - summed * alpha
        normed_ref[:, cols] = ((summed * inv_rms).T * gain_ref[:, cols]).astype(bf16)
        gres_ref[:, cols] = grad_summed.astype(bf16).T
        gq_ref[:, cols] = (grad_summed * mixed).astype(bf16).T


def finish_kernel(
    recv_ref, key_ref, value_ref, gk_hbm, gv_hbm, gf_hbm, gk_ref, gv_ref, gf_ref, sems
):
    tokens, width = key_ref.shape
    peers, rows, _ = recv_ref.shape
    channels = rows // 2
    group = tokens // channels
    parts = sems.shape[0]
    steps = width // tokens // parts
    leaving = []
    for part in range(parts):
        for j in range(part * steps, (part + 1) * steps):
            cols = pl.ds(j * tokens, tokens)
            dest = pl.ds(j * group, group)
            back = recv_ref[dest, :channels, :].reshape(tokens, tokens).T.astype(f32)
            gk_ref[:, cols] = (back * value_ref[:, cols].astype(f32)).astype(bf16)
            gv_ref[:, cols] = (back * key_ref[:, cols].astype(f32)).astype(bf16)
            gf_ref[:, cols] = recv_ref[dest, channels:, :].reshape(tokens, tokens).T.astype(f32)
        cols = pl.ds(part * (width // parts), width // parts)
        pairs = ((gk_ref, gk_hbm), (gv_ref, gv_hbm), (gf_ref, gf_hbm))
        for i, (source, target) in enumerate(pairs):
            leaving.append(
                pltpu.make_async_copy(source.at[:, cols], target.at[:, cols], sems.at[part, i])
            )
            leaving[-1].start()
    for copy in leaving:
        copy.wait()


def places(side, stride, count, step):
    pairs = []
    for source in range(count):
        place = source // stride % side
        pairs.append((source, source + ((place + step) % side - place) * stride))
    return pairs


def add_kernel(*refs):
    *sources, out_ref = refs
    own, *others = (ref[...] for ref in sources)
    out_ref[...] = sum(others, own)


def sum_over(values, axis, side, stride, cost=None):
    count = lax.axis_size(axis)
    moved = [
        lax.ppermute(values, axis, places(side, stride, count, step)) for step in range(1, side)
    ]
    if cost is not None:
        out = shape(values.shape, values.dtype)
        return call(add_kernel, out, n_in=side, cost=cost)(values, *moved)
    for part in moved:
        values = values + part
    return values


def call(kernel, out_shape, n_in, scratch=(), cost=None, smem=(), hbm=(), hbm_out=()):
    def place(i, scalar, far):
        space = pltpu.SMEM if i in scalar else pltpu.HBM if i in far else pltpu.VMEM
        return pl.BlockSpec(memory_space=space)

    outs = out_shape if isinstance(out_shape, tuple) else (out_shape,)
    out_specs = tuple(place(i, (), hbm_out) for i in range(len(outs)))
    return pl.pallas_call(
        kernel,
        out_shape=out_shape,
        in_specs=[place(i, smem, hbm) for i in range(n_in)],
        out_specs=out_specs if isinstance(out_shape, tuple) else out_specs[0],
        scratch_shapes=list(scratch),
        compiler_params=pltpu.CompilerParams(vmem_limit_bytes=48 * 1024 * 1024),
        cost_estimate=cost,
    )


def far_memory(values):
    return pltpu.with_memory_space_constraint(values, pltpu.HBM)


def shape(dims, dtype):
    return jax.ShapeDtypeStruct(dims, dtype)


def run_conv(received, skip_here):
    peers, rows, tokens = received.shape
    channels = rows // 2
    half = channels * peers
    spectra_shape = (2 * half, 2 * tokens)
    vm = pltpu.VMEM
    return call(
        conv_kernel,
        (pltpu.HBM((peers, channels, tokens), bf16), pltpu.HBM(spectra_shape, f32)),
        n_in=7,
        smem=(1,),
        hbm_out=(0, 1),
        scratch=(
            vm(spectra_shape, f32),
            vm((2 * half + 8 * peers, tokens), f32),
            vm((2 * half, 4 * tokens), bf16),
            vm((half, 2 * tokens), f32),
            vm((half + 8 * peers, tokens), f32),
            vm((peers, channels, tokens), bf16),
            pltpu.SemaphoreType.DMA((rows // 4,)),
            pltpu.SemaphoreType.DMA((4,)),
        ),
    )(received, skip_here, *tables(peers, tokens))


def run_lag(received, skip_here, spectra, *after):
    peers, channels, tokens = received.shape
    half = channels * peers
    spectra_shape = (2 * half, 2 * tokens)
    vm = pltpu.VMEM
    return call(
        lag_kernel,
        pltpu.HBM((peers, 2 * channels, tokens), bf16),
        n_in=8 + len(after),
        smem=(1,),
        hbm=(7, 8),
        hbm_out=(0,),
        scratch=(
            vm(spectra_shape, f32),
            vm((half + 8 * peers, tokens), f32),
            vm((half, 2 * tokens), f32),
            vm((2 * half, 4 * tokens), bf16),
            vm(spectra_shape, f32),
            vm((2 * half + 8 * peers, tokens), f32),
            vm((2, peers, channels, tokens), bf16),
            pltpu.SemaphoreType.DMA((channels // 2,)),
            pltpu.SemaphoreType.DMA((2,)),
        ),
    )(received, skip_here, *tables(peers, tokens), far_memory(spectra), *after)


sides = (4, 4, 4)


def on_device(
    residual, query_feats, key_feats, value_feats, filters, cotangent, skip_bias, norm_gain
):
    tokens, width = residual.shape
    peers = lax.axis_size("seq")
    total = float(width * lax.axis_size("chan"))
    channels = width // peers
    vm = pltpu.VMEM

    def exchange(values):
        return lax.all_to_all(values, "seq", split_axis=0, concat_axis=0, tiled=True)

    plain = (tokens, width)
    turned = (width, tokens)
    dma = pltpu.SemaphoreType.DMA
    aside = pl.CostEstimate(flops=10**6, bytes_accessed=4 * 10**6, transcendentals=0)
    parts = 4
    sent = call(
        send_kernel,
        pltpu.HBM((peers, 2 * channels, tokens), bf16),
        n_in=3,
        hbm=(0, 1, 2),
        hbm_out=(0,),
        scratch=(
            vm(plain, bf16),
            vm(plain, bf16),
            vm(plain, bf16),
            vm((peers, 2 * channels, tokens), bf16),
            dma((parts, 3)),
            dma((parts,)),
        ),
    )(far_memory(key_feats), far_memory(value_feats), far_memory(filters))
    received = exchange(sent)
    gain_row = norm_gain[None, :]
    res_t, q_t, sg_t = call(
        turn_kernel,
        (shape(turned, bf16), shape(turned, bf16), shape(turned, f32)),
        n_in=4,
        cost=aside,
    )(residual, query_feats, cotangent, gain_row)
    skip_here = lax.dynamic_slice_in_dim(skip_bias, lax.axis_index("seq") * channels, channels)
    mixed_sent, spectra = run_conv(received, skip_here)
    mixed_t = exchange(mixed_sent).reshape(width, tokens)
    sums = call(sums_kernel, shape((2, tokens), f32), n_in=4)(mixed_t, res_t, q_t, sg_t)
    near = sum_over(sums, "chan", 2, 1)
    far = lax.ppermute(near, "chan", places(2, 2, 4, 1))
    grad_sent = call(
        functools.partial(grad_kernel, total),
        pltpu.HBM(turned, bf16),
        n_in=6,
        hbm_out=(0,),
        scratch=(vm(turned, bf16), dma((parts,))),
    )(near, far, mixed_t, res_t, q_t, sg_t)
    grad_received = exchange(grad_sent.reshape(peers, channels, tokens))
    ends = call(
        functools.partial(ends_kernel, total), shape((2, width), f32), n_in=9, cost=aside
    )(near, far, mixed_t, res_t, q_t, sg_t, cotangent, key_feats, value_feats)
    normed, grad_residual, grad_query = call(
        functools.partial(norm_kernel, total),
        (shape(plain, bf16), shape(plain, bf16), shape(plain, bf16)),
        n_in=7,
        cost=aside,
    )(near, far, mixed_t, res_t, q_t, sg_t, gain_row)
    side_z, side_y, side_x = sides
    ends = sum_over(ends, "seq", side_x, 1)
    lag_sent = run_lag(grad_received, skip_here, spectra, ends)
    late = pl.CostEstimate(flops=3 * 10**10, bytes_accessed=10**8, transcendentals=0)
    plane = side_x * side_y
    ends = sum_over(ends, "seq", 2, side_z // 2 * plane, late)
    ends = sum_over(ends, "seq", side_z // 2, plane)
    ends = sum_over(ends, "seq", side_y, side_x)
    lag_received = exchange(lag_sent)
    grad_key, grad_value, grad_filter = call(
        finish_kernel,
        (shape(plain, bf16), shape(plain, bf16), shape(plain, f32)),
        n_in=3,
        hbm_out=(0, 1, 2),
        scratch=(vm(plain, bf16), vm(plain, bf16), vm(plain, f32), dma((parts, 3))),
    )(lag_received, key_feats, value_feats)
    return (
        normed,
        grad_residual,
        grad_query,
        grad_key,
        grad_value,
        grad_filter,
        ends[0],
        ends[1],
    )


def solution(mesh):
    return jax.shard_map(
        on_device,
        mesh=mesh,
        in_specs=(P("seq", "chan"),) * 6 + (P("chan"),) * 2,
        out_specs=(P("seq", "chan"),) * 6 + (P("chan"),) * 2,
        check_vma=False,
    )
```
